32 devices in a mesh: member: 2 (over y), comp: 2 (over core), tile: 4 (over z), sub: 2 (over x).
Axes of the slice: x: 2, y: 2, z: 4, core: 2. Of those that a mesh axis runs over, the one named last changes fastest.
Arguments:
- tracers: float32 [2, 6, 32, 32, 256], P('comp', 'member', None, 'tile', 'sub'), parts along dimension 1, may hold values from -6 to 6
- couple: float32 [2, 64, 32, 256], P('comp', 'member', 'tile', 'sub'), parts along dimension 1, may hold values from 0.3 to 10
- send_cell: int32 [2, 8, 8, 128], P('comp', ('tile', 'sub')), may hold values from 0 to 1023
- recv_pos: int32 [2, 8, 16384], P('comp', ('tile', 'sub')), may hold values from 0 to 1023, as said below
- row_count: int32 [8], P(('tile', 'sub')), may hold values from 1024 to 16384, as said below
- sea_mask: int32 [8, 16384], P(('tile', 'sub')), may hold values 0 or 1
- exch_coef: float32 [6, 8, 16384], P('member', ('tile', 'sub')), parts along dimension 0, may hold values from 0.3 to 3
- margin_area: float32 [2, 8, 16384], P('comp', ('tile', 'sub')), may hold values from 0.2 to 1
Outputs:
- updated: float32 [2, 6, 32, 32, 256], P('comp', 'member', None, 'tile', 'sub'), parts along dimension 1
The draws below stay inside these ranges and needn't reach their ends.
There are 2 independent parts, one for each index of `member`. The reference program is written for one: setup_inputs(seed, part) draws one part's arguments, and reference() takes and returns one part's arrays. A program takes and returns all parts, laid end to end along the dimension named above; an argument that names none is the same for every part. Nothing has to cross between parts.
Inputs may be any that keep to these rules, and one draw needn't show every extreme that they name: Rows of owner o from row_count[o] on are padding; in every draw some owner holds 16384 live rows. recv_pos[c, o, r] = s * 128 + k names entry k of the list that device s of component c sends to owner o.
All inputs are finite; a program needn't handle non-finite values. No bound on the sum of `sea_mask` on one device may be relied on, other than what follows from the above.
Results may differ from the reference program's by a relative error of at most 0.00002.
Values sent between devices are 32-bit elements; how exact they have to be, the bound alone decides.
A program may use at most 64 MiB of HBM per device.

```python
import math
import jax
import jax.numpy as jnp

NV = 3
LEV = 32
CA = 8
CB = 128
SLOT = 128
ROWS = 16384
OWNERS = 8
NY = 32
NX = 256
N_TILE = 4
N_SUB = 2


def busiest_owner(key):
    return jax.random.randint(jax.random.fold_in(key, 12), (), 0, N_TILE * N_SUB)


def owner_loads(key):
    owners = N_TILE * N_SUB
    powers = jax.random.randint(jax.random.fold_in(key, 11), (owners,), 1, 4)
    loads = jnp.left_shift(jnp.ones((owners,), jnp.int32), powers.astype(jnp.int32))
    busiest = busiest_owner(key)
    return jnp.where(jnp.arange(owners) == busiest, 8, loads)


def draw_row_count(key, part):
    loads = owner_loads(key)
    key = jax.random.fold_in(key, 1)
    removed = jax.random.randint(key, loads.shape, 0, ROWS // 16)
    return jnp.where(loads == 8, ROWS, ROWS * loads // 8 - removed).astype(jnp.int32)


def draw_recv_pos(key, part):
    loads = owner_loads(key)
    busiest = busiest_owner(key)
    key = jax.random.fold_in(key, 2)
    owners = N_TILE * N_SUB
    owner_ids = jnp.arange(owners)
    stacked = []
    for component in range(2):
        key_counts, key_forced, key_source, key_slot = jax.random.split(jax.random.fold_in(key, component), 4)
        capacity = SLOT * loads // 8
        random_counts = jax.random.randint(key_counts, (owners, owners), capacity[:, None] // 2 + 1, 1 + capacity[:, None])
        forced = jax.random.randint(key_forced, (owners,), 0, owners)
        forced = jnp.where(owner_ids == busiest, owners - 1, forced)
        counts = jnp.where(owner_ids[None, :] == forced[:, None], capacity[:, None], random_counts)
        source = jax.random.randint(key_source, (owners, ROWS), 0, owners)
        live_count = jnp.take_along_axis(counts, source, axis=1)
        slot_index = jax.random.randint(key_slot, (owners, ROWS), 0, live_count)
        positions = source * SLOT + slot_index
        first_row = (owner_ids[:, None] == busiest) & (jnp.arange(ROWS)[None, :] == 0)
        positions = jnp.where(first_row, owners * SLOT - 1, positions)
        stacked.append(positions)
    return jnp.stack(stacked).astype(jnp.int32)


def plant(result, key, least, largest):
    dims = result.shape
    index_at = [jax.random.randint(jax.random.fold_in(key, axis), (), 0, dims[axis]) for axis in range(len(dims))]
    result = result.at[tuple(index_at)].set(least)
    longest = dims.index(max(dims))
    index_at[longest] = (index_at[longest] + 1) % dims[longest]
    return result.at[tuple(index_at)].set(largest)


def level_of(key, shape, shards, low, largest):
    gain, own = 1.0, jax.random.fold_in(key, 6)
    for dim, shards_of in shards:
        draws = jnp.exp(jax.random.uniform(jax.random.fold_in(own, dim), (shards_of,), jnp.float32, low / len(shards), largest / len(shards)))
        gain = gain * jnp.repeat(draws, shape[dim] // shards_of).reshape([-1 if axis == dim else 1 for axis in range(len(shape))])
    return gain


def noise(own_key, dims, width, bound, shards=(), held_as=jnp.bfloat16):
    loudness = level_of(own_key, dims, shards, -0.22, 0.18) if shards else 1.0
    drawn = jax.random.normal(own_key, dims, jnp.float32) * width * loudness
    return jnp.minimum(jnp.maximum(drawn, -bound), bound).astype(held_as)


def setup_inputs(seed: int = 0, part: int = 0) -> dict:
    key_list = jax.random.split(jax.random.key(seed), 9)
    part_splits = jax.random.split(jax.random.fold_in(key_list[8], part), 9)
    return {
        "tracers": noise(part_splits[0], (2, NV, LEV, NY, NX), 1.0, 6.0, ((0, 2), (3, 4), (4, 2)), jnp.float32),
        "couple": jnp.clip(jnp.exp(math.log(10.0) - 3.506558 * jax.random.uniform(part_splits[1], (2, LEV, NY, NX), jnp.float32) ** level_of(part_splits[1], (2, LEV, NY, NX), ((0, 2), (2, 4), (3, 2)), -0.2, 0.2)), 0.3, 10.0),
        "send_cell": plant(jax.random.randint(key_list[2], (2, OWNERS, OWNERS, SLOT), 0, CA * CB), jax.random.fold_in(key_list[2], 1), 0, (CA * CB) - 1).astype(jnp.int32),
        "recv_pos": draw_recv_pos(jax.random.fold_in(key_list[8], 71), part),
        "row_count": draw_row_count(jax.random.fold_in(key_list[8], 71), part),
        "sea_mask": plant((jax.random.randint(key_list[5], (OWNERS, ROWS), 0, 4) < 3).astype(jnp.int32), jax.random.fold_in(key_list[5], 1), 0, 1),
        "exch_coef": jnp.clip(jnp.exp(math.log(3.0) - 2.3025851 * jax.random.uniform(part_splits[6], (NV, OWNERS, ROWS), jnp.float32) ** level_of(part_splits[6], (NV, OWNERS, ROWS), ((1, 8),), -0.2, 0.2)), 0.3, 3.0),
        "margin_area": jnp.clip(0.2 + 0.8 * jax.random.uniform(key_list[7], (2, OWNERS, ROWS), jnp.float32) ** level_of(key_list[7], (2, OWNERS, ROWS), ((0, 2), (1, 8)), -0.2, 0.2), 0.2, 1.0),
    }


SMOOTH_RATE = 0.2


def laplace(field):
    padded = jnp.pad(field, [(0, 0)] * (field.ndim - 2) + [(1, 1), (1, 1)])
    beside_all = padded[..., 2:, 1:-1] + padded[..., :-2, 1:-1] + padded[..., 1:-1, 2:] + padded[..., 1:-1, :-2]
    return beside_all - 4.0 * field


def reference(tracers, couple, send_cell, recv_pos, row_count, sea_mask, exch_coef, margin_area):
    zeros_plane = jnp.zeros_like(couple[:, 0])
    offsets = []
    factors = []
    for level in range(LEV):
        couple_above = couple[:, level]
        couple_below = couple[:, level + 1] if level + 1 < LEV else zeros_plane
        if level == 0:
            pivot = 1.0 + couple_above + couple_below
            offset_now = tracers[:, :, 0] / pivot[:, None]
        else:
            pivot = 1.0 + couple_above + couple_below - couple_above * factors[-1]
            offset_now = (tracers[:, :, level] + couple_above[:, None] * offsets[-1]) / pivot[:, None]
        offsets.append(offset_now)
        factors.append(couple_below / pivot)
    surface_e = offsets[-1]
    surface_f = 1.0 / pivot
    packed = jnp.concatenate([surface_e, surface_f[:, None]], axis=1)
    per_device = packed.reshape(2, NV + 1, N_TILE, CA, N_SUB, CB).transpose(0, 2, 4, 3, 5, 1)
    per_device = per_device.reshape(2, N_TILE * N_SUB, CA * CB, NV + 1)
    sources = recv_pos // SLOT
    slot_index = recv_pos % SLOT
    owner_ids = jnp.arange(N_TILE * N_SUB, dtype=jnp.int32)[None, :, None]
    component = jnp.arange(2, dtype=jnp.int32)[:, None, None]
    cells = send_cell[component, sources, owner_ids, slot_index]
    values = per_device[component, sources, cells]
    other = values[::-1]
    coef = jnp.moveaxis(exch_coef, 0, -1)[None]
    live = ((jnp.arange(ROWS, dtype=jnp.int32)[None, :] < row_count[:, None]) & (sea_mask == 1)).astype(jnp.float32)
    weight = live[None] * margin_area
    flux = coef * (other[..., :NV] - values[..., :NV]) / (1.0 + coef * (values[..., NV:] + other[..., NV:]))
    flux = flux * weight[..., None]
    target = (component * (N_TILE * N_SUB) + sources) * (CA * CB) + cells
    cell_flux = jax.ops.segment_sum(flux.reshape(-1, NV), target.reshape(-1), num_segments=2 * N_TILE * N_SUB * CA * CB)
    cell_flux = cell_flux.reshape(2, N_TILE, N_SUB, CA, CB, NV).transpose(0, 5, 1, 3, 2, 4)
    cell_flux = cell_flux.reshape(2, NV, N_TILE * CA, N_SUB * CB)
    column = surface_e + surface_f[:, None] * cell_flux
    stacked = [column]
    for level in range(LEV - 2, -1, -1):
        column = offsets[level] + factors[level][:, None] * column
        stacked.append(column)
    vertical = jnp.stack(stacked[::-1], axis=2)
    smooth_once = tracers + SMOOTH_RATE * laplace(tracers)
    smooth_twice = smooth_once + SMOOTH_RATE * laplace(smooth_once)
    return vertical + (smooth_twice - tracers)
```

```python
import functools
import jax
import jax.numpy as jnp
from jax import lax
from jax.experimental import pallas as pl
from jax.experimental.pallas import tpu as pltpu
from jax.sharding import PartitionSpec as P

SMOOTH_RATE = 0.2
LANES = 128
SUBS = 8
MESH = pl.DeviceIdType.MESH
F32 = jnp.float32
BF16 = jnp.bfloat16


def lane_gather(table, index):
    return jnp.take_along_axis(table, index, axis=1, mode="promise_in_bounds")


def row_of(value, row, rows):
    return jnp.broadcast_to(value[row : row + 1], (rows, value.shape[1]))


def one_hot(low_row):
    spread = jnp.broadcast_to(low_row.astype(F32), (16, LANES)).astype(BF16)
    base = lax.broadcasted_iota(jnp.int32, (16, LANES), 0)
    one, zero = (jnp.full((16, LANES), value, BF16) for value in (1.0, 0.0))
    return jnp.concatenate(
        [
            jnp.where((base + 16 * k).astype(F32).astype(BF16) == spread, one, zero)
            for k in range(LANES // 16)
        ],
        axis=0,
    )


def contract_lanes(a, b):
    return lax.dot_general(a, b, (((1,), (1,)), ((), ())), preferred_element_type=F32)


def kernel(
    n_tile, n_sub, nvar, nlev,
    tr, couple, send_cell, pos, row_count, sea, coef, area,
    out,
    off, fac, once, dif, tab_out, tab_in, tabs, posb, areab, wgt, acc, ret_out, ret_in,
    row_s, row_r, col_s, col_r, cells,
    part_sem, halo_send, halo_recv, list_sem,
):
    owners = n_tile * n_sub
    groups = owners // SUBS
    tiles = nvar * nlev
    slab = tiles // SUBS
    half = pos.shape[0] // 2
    devices = 2 * owners
    comp, tile, sub = lax.axis_index("comp"), lax.axis_index("tile"), lax.axis_index("sub")
    me_owner = tile * n_sub + sub
    me = comp * owners + me_owner

    def place(index):
        owner = index % owners
        return {"comp": index // owners, "tile": owner // n_sub, "sub": owner % n_sub}

    barrier = pltpu.get_barrier_semaphore()

    def greet(step, carry):
        pl.semaphore_signal(
            barrier, inc=1, device_id=place((me + step) % devices), device_id_type=MESH
        )
        return carry

    lax.fori_loop(1, devices, greet, 0)

    factor = None
    offset = [None] * nvar
    for level in range(nlev):
        above = couple[level]
        below = couple[level + 1] if level + 1 < nlev else jnp.zeros_like(above)
        pivot = 1.0 + above + below
        if level > 0:
            pivot = pivot - above * factor
        inverse = 1.0 / pivot
        for var in range(nvar):
            right = tr[var * nlev + level]
            if level > 0:
                right = right + above * offset[var]
            offset[var] = right * inverse
            off[var * nlev + level] = offset[var]
        factor = below * inverse
        fac[level] = factor
    surface = offset + [inverse]

    def make_lists(group, carry):
        start = pl.multiple_of(group * SUBS, SUBS)
        cell = send_cell[pl.ds(start, SUBS), :]
        low, high = cell & (LANES - 1), cell >> 7
        for var in range(nvar + 1):
            value = jnp.zeros((SUBS, LANES), F32)
            for a in range(SUBS):
                found = lane_gather(row_of(surface[var], a, SUBS), low)
                value = jnp.where(high == a, found, value)
            for o in range(SUBS):
                tab_out[start + o, var : var + 1, :] = value[o : o + 1]
        return carry

    def loop(count, body, carry):
        if count == 1:
            return body(0, carry)
        return lax.fori_loop(0, count, body, carry)

    loop(groups, make_lists, 0)
    tab_in[me] = tab_out[me_owner]

    pl.semaphore_wait(barrier, devices - 1)

    other_half = pl.multiple_of((1 - comp) * half, half)
    my_half = pl.multiple_of(comp * half, half)
    partner = {"comp": 1 - comp}
    part_copies = [
        pltpu.make_async_remote_copy(
            src_ref=source.at[pl.ds(other_half, half)],
            dst_ref=target.at[comp],
            send_sem=part_sem.at[2 * k],
            recv_sem=part_sem.at[2 * k + 1],
            device_id=partner,
            device_id_type=MESH,
        )
        for k, (source, target) in enumerate(((pos, posb), (area, areab)))
    ]

    def spread_lists(source, target, send, recv, by_owner):
        def body(step, carry):
            to = (me + step) % devices
            pltpu.make_async_remote_copy(
                src_ref=source.at[to % owners if by_owner else to],
                dst_ref=target.at[me],
                send_sem=list_sem.at[send],
                recv_sem=list_sem.at[recv],
                device_id=place(to),
                device_id_type=MESH,
            ).start()
            return carry

        lax.fori_loop(1, devices, body, 0)

    def wait_lists(target, sem):
        whole = target.at[pl.ds(0, devices - 1)]
        pltpu.make_async_copy(whole, whole, list_sem.at[sem]).wait()

    spread_lists(tab_out, tab_in, 0, 1, True)
    for copy in part_copies:
        copy.start()

    sub_iota = lax.broadcasted_iota(jnp.int32, (slab, SUBS, LANES), 1)
    lane_iota = lax.broadcasted_iota(jnp.int32, (slab, SUBS, LANES), 2)
    tile_iota = lax.broadcasted_iota(jnp.int32, (slab, SUBS, LANES), 0)

    def turn(value, shift, axis):
        return value if shift == 0 else pltpu.roll(value, shift, axis)

    links = (
        (row_s, row_r, 0, tile > 0, tile < n_tile - 1, "tile", tile),
        (col_s, col_r, 2, sub > 0, sub < n_sub - 1, "sub", sub),
    )

    def halo_copy(turn_no, link, side):
        sends, receives, base, _, _, axis, place_at = link
        return pltpu.make_async_remote_copy(
            src_ref=sends.at[turn_no, side],
            dst_ref=receives.at[turn_no, 1 - side],
            send_sem=halo_send.at[turn_no, base + side],
            recv_sem=halo_recv.at[turn_no, base + 1 - side],
            device_id={axis: place_at + (1 if side else -1)},
            device_id_type=MESH,
        )

    def send_halos(turn_no, source):
        first = jnp.zeros((slab, SUBS, LANES), F32)
        last = first
        col_first = jnp.zeros((SUBS, LANES), F32)
        col_last = col_first
        for j in range(SUBS):
            block = source[j * slab : (j + 1) * slab]
            first = jnp.where(sub_iota == j, turn(block, j, 1), first)
            last = jnp.where(sub_iota == j, turn(block, (j + 1) % SUBS, 1), last)
            here = lane_iota == tile_iota + j * slab
            shape = (slab, SUBS, LANES)
            left = jnp.broadcast_to(block[:, :, 0:1], shape)
            right = jnp.broadcast_to(block[:, :, LANES - 1 : LANES], shape)
            col_first = col_first + jnp.sum(jnp.where(here, left, 0.0), axis=0)
            col_last = col_last + jnp.sum(jnp.where(here, right, 0.0), axis=0)
        row_s[turn_no, 0] = first
        row_s[turn_no, 1] = last
        col_s[turn_no, 0] = col_first
        col_s[turn_no, 1] = col_last
        for link in links:
            for side in range(2):
                receives, there = link[1], link[3 + side]

                @pl.when(there)
                def _():
                    halo_copy(turn_no, link, side).start()

                @pl.when(jnp.logical_not(there))
                def _():
                    receives[turn_no, side] = jnp.zeros(receives.shape[2:], F32)

    def wait_halos(turn_no):
        for link in links:
            for side in range(2):

                @pl.when(link[3 + side])
                def _():
                    halo_copy(turn_no, link, 1 - side).wait_recv()

    def finish_halos(turn_no):
        for link in links:
            for side in range(2):

                @pl.when(link[3 + side])
                def _():
                    halo_copy(turn_no, link, side).wait_send()

    def smooth(turn_no, source, target, subtract):
        up_rows, down_rows = row_r[turn_no, 0], row_r[turn_no, 1]
        left_cols, right_cols = (
            jnp.broadcast_to(col_r[turn_no, side][None], (slab, SUBS, LANES)).reshape(
                slab * SUBS, LANES
            )
            for side in range(2)
        )
        for j in range(SUBS):
            block = source[j * slab : (j + 1) * slab]
            at = (tile_iota + j * slab).reshape(slab * SUBS, LANES)
            left_halo = lane_gather(left_cols, at).reshape(slab, SUBS, LANES)
            right_halo = lane_gather(right_cols, at).reshape(slab, SUBS, LANES)
            up = jnp.where(sub_iota == 0, turn(up_rows, (SUBS - j) % SUBS, 1), turn(block, 1, 1))
            down = jnp.where(
                sub_iota == SUBS - 1, turn(down_rows, SUBS - 1 - j, 1), turn(block, SUBS - 1, 1)
            )
            left = jnp.where(lane_iota == 0, left_halo, turn(block, 1, 2))
            right = jnp.where(lane_iota == LANES - 1, right_halo, turn(block, LANES - 1, 2))
            result = block + SMOOTH_RATE * ((down + up + right + left) - 4.0 * block)
            if subtract is not None:
                result = result - subtract[j * slab : (j + 1) * slab]
            target[j * slab : (j + 1) * slab] = result

    send_halos(0, tr)

    posb[comp] = pos[pl.ds(my_half, half), :]
    areab[comp] = area[pl.ds(my_half, half), :]

    wait_halos(0)
    smooth(0, tr, once, None)
    send_halos(1, once)

    for copy in part_copies:
        copy.wait_recv()
    row_number = (
        (lax.broadcasted_iota(jnp.int32, (half, LANES), 0) + my_half) * LANES
        + lax.broadcasted_iota(jnp.int32, (half, LANES), 1)
    )
    live = (row_number < row_count[0]) & (sea[pl.ds(my_half, half), :] == 1)
    for c in range(2):
        wgt[c] = jnp.where(live, areab[c], 0.0)

    wait_lists(tab_in, 1)
    sub8 = lax.broadcasted_iota(jnp.int32, (SUBS, LANES), 0)
    upper = sub8 < 4
    quarter = sub8 & 3

    def join_tables(s, carry):
        tabs[s] = jnp.concatenate([tab_in[s], tab_in[owners + s]], axis=0)
        return carry

    if groups == 1:
        for s in range(owners):
            join_tables(s, 0)
    else:
        lax.fori_loop(0, owners, join_tables, 0)
    acc[...] = jnp.zeros_like(acc)

    def rows_step(step, carry):
        start = pl.multiple_of(step * SUBS, SUBS)
        at = pl.ds(start, SUBS)
        at_half = pl.ds(pl.multiple_of(my_half + step * SUBS, SUBS), SUBS)
        places = [posb[c, at, :] for c in range(2)]
        weights = [wgt[c, at, :] for c in range(2)]
        coefs = [coef[v, at_half, :] for v in range(nvar)]
        lows, highs, hots = [], [], [[], []]
        for j in range(SUBS):
            p = jnp.where(upper, row_of(places[0], j, SUBS), row_of(places[1], j, SUBS))
            lows.append(p & (LANES - 1))
            highs.append(p >> 7)
            for c in range(2):
                hots[c].append(one_hot((places[c] & (LANES - 1))[j : j + 1]))

        def find(group, found):
            found = list(found)
            for k in range(SUBS):
                s = group * SUBS + k
                table = tabs[s]
                for j in range(SUBS):
                    found[j] = jnp.where(highs[j] == s, lane_gather(table, lows[j]), found[j])
            return tuple(found)

        found = loop(groups, find, tuple(jnp.zeros((SUBS, LANES), F32) for _ in range(SUBS)))
        terms, sources = [], []
        for j in range(SUBS):
            own = found[j]
            other = pltpu.roll(own, 4, 0)
            k = row_of(coefs[nvar - 1], j, SUBS)
            for v in range(nvar - 1):
                k = jnp.where(quarter == v, row_of(coefs[v], j, SUBS), k)
            w = jnp.where(upper, row_of(weights[0], j, SUBS), row_of(weights[1], j, SUBS))
            both = row_of(own + other, nvar, SUBS)
            flux = k * (other - own) / (1.0 + k * both) * w
            main = flux.astype(BF16).astype(F32)
            terms.append(jnp.concatenate([main, flux - main], axis=0).astype(BF16))
            sources.append(
                jnp.concatenate([highs[j], highs[j]], axis=0).astype(F32).astype(BF16)
            )
        hot = [jnp.concatenate(hots[c], axis=1) for c in range(2)]

        def add(group, carry):
            none = jnp.zeros((16, LANES), BF16)
            columns = []
            for j in range(SUBS):
                columns.append(
                    jnp.concatenate(
                        [
                            jnp.where(
                                sources[j]
                                == jnp.full((16, LANES), group * SUBS + k, jnp.int32)
                                .astype(F32)
                                .astype(BF16),
                                terms[j],
                                none,
                            )
                            for k in range(SUBS)
                        ],
                        axis=0,
                    )
                )
            a = jnp.concatenate(columns, axis=1)
            for c in range(2):
                acc[c, group] += contract_lanes(a, hot[c])
            return carry

        loop(groups, add, 0)
        return carry

    lax.fori_loop(0, half // SUBS, rows_step, 0)

    def give_back(group, carry):
        for c in range(2):
            for k in range(SUBS):
                base = 16 * k + 4 * c
                total = acc[c, group, base : base + 4, :] + acc[c, group, base + 8 : base + 12, :]
                ret_out[c * owners + group * SUBS + k] = total
        return carry

    loop(groups, give_back, 0)
    ret_in[me] = ret_out[me]
    spread_lists(ret_out, ret_in, 2, 3, False)

    wait_halos(1)
    smooth(1, once, dif, tr)

    cells[...] = jnp.zeros_like(cells)
    wait_lists(ret_in, 3)

    def cells_step(group, carry):
        start = pl.multiple_of(group * SUBS, SUBS)
        cell = send_cell[pl.ds(start, SUBS), :]
        low, high = cell & (LANES - 1), cell >> 7
        columns, hot = [], []
        for j in range(SUBS):
            value = ret_in[start + j] + ret_in[owners + start + j]
            mask = row_of(high, j, SUBS) == sub8
            hot.append(one_hot(low[j : j + 1]))
            parts = []
            for _ in range(3):
                part = value.astype(BF16).astype(F32)
                value = value - part
                for v in range(4):
                    parts.append(jnp.where(mask, row_of(part, v, SUBS), 0.0))
            columns.append(jnp.concatenate(parts, axis=0).astype(BF16))
        cells[...] += contract_lanes(
            jnp.concatenate(columns, axis=1), jnp.concatenate(hot, axis=1)
        )
        return carry

    loop(groups, cells_step, 0)
    for var in range(nvar):
        parts = [cells[32 * k + 8 * var : 32 * k + 8 * var + 8, :] for k in range(3)]
        flux = parts[0] + (parts[1] + parts[2])
        last = var * nlev + nlev - 1
        column = surface[var] + surface[nvar] * flux
        out[last] = column + dif[last]
        for level in range(nlev - 2, -1, -1):
            n = var * nlev + level
            column = off[n] + fac[level] * column
            out[n] = column + dif[n]

    for copy in part_copies:
        copy.wait_send()
    finish_halos(0)
    finish_halos(1)
    wait_lists(tab_in, 0)
    wait_lists(ret_in, 2)


def per_device(
    n_tile, n_sub, tracers, couple, send_cell, recv_pos, row_count, sea_mask, exch_coef, margin_area
):
    nvar, nlev = tracers.shape[1:3]
    tiles = nvar * nlev
    owners = n_tile * n_sub
    rows = recv_pos.shape[-1] // LANES
    slab = tiles // SUBS
    block = (SUBS, LANES)
    vmem = pl.BlockSpec(memory_space=pltpu.VMEM)
    scratch = [
        pltpu.VMEM((tiles,) + block, F32),
        pltpu.VMEM((nlev,) + block, F32),
        pltpu.VMEM((tiles,) + block, F32),
        pltpu.VMEM((tiles,) + block, F32),
        pltpu.VMEM((owners, 4, LANES), F32),
        pltpu.VMEM((2 * owners, 4, LANES), F32),
        pltpu.VMEM((owners,) + block, F32),
        pltpu.VMEM((2, rows // 2, LANES), jnp.int32),
        pltpu.VMEM((2, rows // 2, LANES), F32),
        pltpu.VMEM((2, rows // 2, LANES), F32),
        pltpu.VMEM((2, owners // SUBS, 16 * SUBS, LANES), F32),
        pltpu.VMEM((2 * owners, 4, LANES), F32),
        pltpu.VMEM((2 * owners, 4, LANES), F32),
        pltpu.VMEM((2, 2, slab) + block, F32),
        pltpu.VMEM((2, 2, slab) + block, F32),
        pltpu.VMEM((2, 2) + block, F32),
        pltpu.VMEM((2, 2) + block, F32),
        pltpu.VMEM((96, LANES), F32),
        pltpu.SemaphoreType.DMA((4,)),
        pltpu.SemaphoreType.DMA((2, 4)),
        pltpu.SemaphoreType.DMA((2, 4)),
        pltpu.SemaphoreType.DMA((4,)),
    ]
    updated = pl.pallas_call(
        functools.partial(kernel, n_tile, n_sub, nvar, nlev),
        out_shape=jax.ShapeDtypeStruct((tiles,) + block, F32),
        in_specs=[vmem] * 4 + [pl.BlockSpec(memory_space=pltpu.SMEM)] + [vmem] * 3,
        out_specs=vmem,
        scratch_shapes=scratch,
        compiler_params=pltpu.CompilerParams(
            collective_id=0, has_side_effects=True, vmem_limit_bytes=32 * 1024 * 1024
        ),
        name="coupled_step",
    )(
        tracers.reshape((tiles,) + block),
        couple.reshape((nlev,) + block),
        send_cell.reshape(owners, LANES),
        recv_pos.reshape(rows, LANES),
        row_count,
        sea_mask.reshape(rows, LANES),
        exch_coef.reshape(nvar, rows, LANES),
        margin_area.reshape(rows, LANES),
    )
    return updated.reshape(tracers.shape)


def solution(mesh):
    placed = (
        P("comp", "member", None, "tile", "sub"),
        P("comp", "member", "tile", "sub"),
        P("comp", ("tile", "sub"), None, None),
        P("comp", ("tile", "sub"), None),
        P(("tile", "sub")),
        P(("tile", "sub"), None),
        P("member", ("tile", "sub"), None),
        P("comp", ("tile", "sub"), None),
    )
    return jax.shard_map(
        functools.partial(per_device, mesh.shape["tile"], mesh.shape["sub"]),
        mesh=mesh,
        in_specs=placed,
        out_specs=P("comp", "member", None, "tile", "sub"),
        check_vma=False,
    )
```

```python
import functools
import jax
import jax.numpy as jnp
from jax import lax
from jax.experimental import pallas as pl
from jax.experimental.pallas import tpu as pltpu
from jax.sharding import PartitionSpec as P

SMOOTH_RATE = 0.2
LANES = 128
SUBS = 8
MESH = pl.DeviceIdType.MESH
F32 = jnp.float32
BF16 = jnp.bfloat16


def lane_gather(table, index):
    return jnp.take_along_axis(table, index, axis=1, mode="promise_in_bounds")


def row_of(value, row, rows):
    return jnp.broadcast_to(value[row : row + 1], (rows, value.shape[1]))


def one_hot(low_row):
    spread = jnp.broadcast_to(low_row.astype(F32), (16, LANES)).astype(BF16)
    base = lax.broadcasted_iota(jnp.int32, (16, LANES), 0)
    one, zero = (jnp.full((16, LANES), value, BF16) for value in (1.0, 0.0))
    return jnp.concatenate(
        [
            jnp.where((base + 16 * k).astype(F32).astype(BF16) == spread, one, zero)
            for k in range(LANES // 16)
        ],
        axis=0,
    )


def contract_lanes(a, b):
    return lax.dot_general(a, b, (((1,), (1,)), ((), ())), preferred_element_type=F32)


def kernel(
    n_tile, n_sub, nvar, nlev,
    tr_hbm, couple_hbm, cell_hbm, pos, row_count, sea_hbm, coef_hbm, area,
    out,
    tr, couple, send_cell, sea, coef, load_sem,
    off, fac, once, dif, tab_out, tab_in, tabs, posb, areab, wgt, acc, ret_out, ret_in,
    row_s, row_r, col_s, col_r, cells,
    part_sem, halo_send, halo_recv, list_sem,
):
    owners = n_tile * n_sub
    groups = owners // SUBS
    tiles = nvar * nlev
    slab = tiles // SUBS
    half = pos.shape[0] // 2
    devices = 2 * owners
    comp, tile, sub = lax.axis_index("comp"), lax.axis_index("tile"), lax.axis_index("sub")
    me_owner = tile * n_sub + sub
    me = comp * owners + me_owner

    other_half = pl.multiple_of((1 - comp) * half, half)
    my_half = pl.multiple_of(comp * half, half)
    mine = pl.ds(my_half, half)
    loads = [
        pltpu.make_async_copy(source, target, load_sem.at[k])
        for k, (source, target) in enumerate(
            (
                (couple_hbm, couple),
                (tr_hbm, tr),
                (cell_hbm, send_cell),
                (pos.at[mine], posb.at[comp]),
                (area.at[mine], areab.at[comp]),
                (sea_hbm.at[mine], sea),
                (coef_hbm.at[:, mine], coef),
            )
        )
    ]
    for copy in loads:
        copy.start()

    def place(index):
        owner = index % owners
        return {"comp": index // owners, "tile": owner // n_sub, "sub": owner % n_sub}

    barrier = pltpu.get_barrier_semaphore()

    def greet(step, carry):
        pl.semaphore_signal(
            barrier, inc=1, device_id=place((me + step) % devices), device_id_type=MESH
        )
        return carry

    lax.fori_loop(1, devices, greet, 0)

    loads[0].wait()
    loads[1].wait()
    factor = None
    offset = [None] * nvar
    for level in range(nlev):
        above = couple[level]
        below = couple[level + 1] if level + 1 < nlev else jnp.zeros_like(above)
        pivot = 1.0 + above + below
        if level > 0:
            pivot = pivot - above * factor
        inverse = 1.0 / pivot
        for var in range(nvar):
            right = tr[var * nlev + level]
            if level > 0:
                right = right + above * offset[var]
            offset[var] = right * inverse
            off[var * nlev + level] = offset[var]
        factor = below * inverse
        fac[level] = factor
    surface = offset + [inverse]

    loads[2].wait()

    def make_lists(group, carry):
        start = pl.multiple_of(group * SUBS, SUBS)
        cell = send_cell[pl.ds(start, SUBS), :]
        low, high = cell & (LANES - 1), cell >> 7
        for var in range(nvar + 1):
            value = jnp.zeros((SUBS, LANES), F32)
            for a in range(SUBS):
                found = lane_gather(row_of(surface[var], a, SUBS), low)
                value = jnp.where(high == a, found, value)
            for o in range(SUBS):
                tab_out[start + o, var : var + 1, :] = value[o : o + 1]
        return carry

    def loop(count, body, carry):
        if count == 1:
            return body(0, carry)
        return lax.fori_loop(0, count, body, carry)

    loop(groups, make_lists, 0)
    tab_in[me] = tab_out[me_owner]

    pl.semaphore_wait(barrier, devices - 1)

    partner = {"comp": 1 - comp}
    part_copies = [
        pltpu.make_async_remote_copy(
            src_ref=source.at[pl.ds(other_half, half)],
            dst_ref=target.at[comp],
            send_sem=part_sem.at[2 * k],
            recv_sem=part_sem.at[2 * k + 1],
            device_id=partner,
            device_id_type=MESH,
        )
        for k, (source, target) in enumerate(((pos, posb), (area, areab)))
    ]

    def spread_lists(source, target, send, recv, by_owner):
        def body(step, carry):
            to = (me + step) % devices
            pltpu.make_async_remote_copy(
                src_ref=source.at[to % owners if by_owner else to],
                dst_ref=target.at[me],
                send_sem=list_sem.at[send],
                recv_sem=list_sem.at[recv],
                device_id=place(to),
                device_id_type=MESH,
            ).start()
            return carry

        lax.fori_loop(1, devices, body, 0)

    def wait_lists(target, sem):
        whole = target.at[pl.ds(0, devices - 1)]
        pltpu.make_async_copy(whole, whole, list_sem.at[sem]).wait()

    spread_lists(tab_out, tab_in, 0, 1, True)
    for copy in part_copies:
        copy.start()

    sub_iota = lax.broadcasted_iota(jnp.int32, (slab, SUBS, LANES), 1)
    lane_iota = lax.broadcasted_iota(jnp.int32, (slab, SUBS, LANES), 2)
    tile_iota = lax.broadcasted_iota(jnp.int32, (slab, SUBS, LANES), 0)

    def turn(value, shift, axis):
        return value if shift == 0 else pltpu.roll(value, shift, axis)

    links = (
        (row_s, row_r, 0, tile > 0, tile < n_tile - 1, "tile", tile),
        (col_s, col_r, 2, sub > 0, sub < n_sub - 1, "sub", sub),
    )

    def halo_copy(turn_no, link, side):
        sends, receives, base, _, _, axis, place_at = link
        return pltpu.make_async_remote_copy(
            src_ref=sends.at[turn_no, side],
            dst_ref=receives.at[turn_no, 1 - side],
            send_sem=halo_send.at[turn_no, base + side],
            recv_sem=halo_recv.at[turn_no, base + 1 - side],
            device_id={axis: place_at + (1 if side else -1)},
            device_id_type=MESH,
        )

    def send_halos(turn_no, source):
        first = jnp.zeros((slab, SUBS, LANES), F32)
        last = first
        col_first = jnp.zeros((SUBS, LANES), F32)
        col_last = col_first
        for j in range(SUBS):
            block = source[j * slab : (j + 1) * slab]
            first = jnp.where(sub_iota == j, turn(block, j, 1), first)
            last = jnp.where(sub_iota == j, turn(block, (j + 1) % SUBS, 1), last)
            here = lane_iota == tile_iota + j * slab
            shape = (slab, SUBS, LANES)
            left = jnp.broadcast_to(block[:, :, 0:1], shape)
            right = jnp.broadcast_to(block[:, :, LANES - 1 : LANES], shape)
            col_first = col_first + jnp.sum(jnp.where(here, left, 0.0), axis=0)
            col_last = col_last + jnp.sum(jnp.where(here, right, 0.0), axis=0)
        row_s[turn_no, 0] = first
        row_s[turn_no, 1] = last
        col_s[turn_no, 0] = col_first
        col_s[turn_no, 1] = col_last
        for link in links:
            for side in range(2):
                receives, there = link[1], link[3 + side]

                @pl.when(there)
                def _():
                    halo_copy(turn_no, link, side).start()

                @pl.when(jnp.logical_not(there))
                def _():
                    receives[turn_no, side] = jnp.zeros(receives.shape[2:], F32)

    def wait_halos(turn_no):
        for link in links:
            for side in range(2):

                @pl.when(link[3 + side])
                def _():
                    halo_copy(turn_no, link, 1 - side).wait_recv()

    def finish_halos(turn_no):
        for link in links:
            for side in range(2):

                @pl.when(link[3 + side])
                def _():
                    halo_copy(turn_no, link, side).wait_send()

    def smooth(turn_no, source, target, subtract):
        up_rows, down_rows = row_r[turn_no, 0], row_r[turn_no, 1]
        left_cols, right_cols = (
            jnp.broadcast_to(col_r[turn_no, side][None], (slab, SUBS, LANES)).reshape(
                slab * SUBS, LANES
            )
            for side in range(2)
        )
        for j in range(SUBS):
            block = source[j * slab : (j + 1) * slab]
            at = (tile_iota + j * slab).reshape(slab * SUBS, LANES)
            left_halo = lane_gather(left_cols, at).reshape(slab, SUBS, LANES)
            right_halo = lane_gather(right_cols, at).reshape(slab, SUBS, LANES)
            up = jnp.where(sub_iota == 0, turn(up_rows, (SUBS - j) % SUBS, 1), turn(block, 1, 1))
            down = jnp.where(
                sub_iota == SUBS - 1, turn(down_rows, SUBS - 1 - j, 1), turn(block, SUBS - 1, 1)
            )
            left = jnp.where(lane_iota == 0, left_halo, turn(block, 1, 2))
            right = jnp.where(lane_iota == LANES - 1, right_halo, turn(block, LANES - 1, 2))
            result = block + SMOOTH_RATE * ((down + up + right + left) - 4.0 * block)
            if subtract is not None:
                result = result - subtract[j * slab : (j + 1) * slab]
            target[j * slab : (j + 1) * slab] = result

    send_halos(0, tr)

    wait_halos(0)
    smooth(0, tr, once, None)
    send_halos(1, once)

    for copy in loads[3:]:
        copy.wait()
    for copy in part_copies:
        copy.wait_recv()
    row_number = (
        (lax.broadcasted_iota(jnp.int32, (half, LANES), 0) + my_half) * LANES
        + lax.broadcasted_iota(jnp.int32, (half, LANES), 1)
    )
    live = (row_number < row_count[0]) & (sea[...] == 1)
    for c in range(2):
        wgt[c] = jnp.where(live, areab[c], 0.0)

    wait_lists(tab_in, 1)
    sub8 = lax.broadcasted_iota(jnp.int32, (SUBS, LANES), 0)
    upper = sub8 < 4
    quarter = sub8 & 3

    def join_tables(s, carry):
        tabs[s] = jnp.concatenate([tab_in[s], tab_in[owners + s]], axis=0)
        return carry

    if groups == 1:
        for s in range(owners):
            join_tables(s, 0)
    else:
        lax.fori_loop(0, owners, join_tables, 0)
    acc[...] = jnp.zeros_like(acc)

    def rows_step(step, carry):
        start = pl.multiple_of(step * SUBS, SUBS)
        at = pl.ds(start, SUBS)
        places = [posb[c, at, :] for c in range(2)]
        weights = [wgt[c, at, :] for c in range(2)]
        coefs = [coef[v, at, :] for v in range(nvar)]
        lows, highs, hots = [], [], [[], []]
        for j in range(SUBS):
            p = jnp.where(upper, row_of(places[0], j, SUBS), row_of(places[1], j, SUBS))
            lows.append(p & (LANES - 1))
            highs.append(p >> 7)
            for c in range(2):
                hots[c].append(one_hot((places[c] & (LANES - 1))[j : j + 1]))

        def find(group, found):
            found = list(found)
            for k in range(SUBS):
                s = group * SUBS + k
                table = tabs[s]
                for j in range(SUBS):
                    found[j] = jnp.where(highs[j] == s, lane_gather(table, lows[j]), found[j])
            return tuple(found)

        found = loop(groups, find, tuple(jnp.zeros((SUBS, LANES), F32) for _ in range(SUBS)))
        terms, sources = [], []
        for j in range(SUBS):
            own = found[j]
            other = pltpu.roll(own, 4, 0)
            k = row_of(coefs[nvar - 1], j, SUBS)
            for v in range(nvar - 1):
                k = jnp.where(quarter == v, row_of(coefs[v], j, SUBS), k)
            w = jnp.where(upper, row_of(weights[0], j, SUBS), row_of(weights[1], j, SUBS))
            both = row_of(own + other, nvar, SUBS)
            flux = k * (other - own) / (1.0 + k * both) * w
            main = flux.astype(BF16).astype(F32)
            terms.append(jnp.concatenate([main, flux - main], axis=0).astype(BF16))
            sources.append(
                jnp.concatenate([highs[j], highs[j]], axis=0).astype(F32).astype(BF16)
            )
        hot = [jnp.concatenate(hots[c], axis=1) for c in range(2)]

        def add(group, carry):
            none = jnp.zeros((16, LANES), BF16)
            columns = []
            for j in range(SUBS):
                columns.append(
                    jnp.concatenate(
                        [
                            jnp.where(
                                sources[j]
                                == jnp.full((16, LANES), group * SUBS + k, jnp.int32)
                                .astype(F32)
                                .astype(BF16),
                                terms[j],
                                none,
                            )
                            for k in range(SUBS)
                        ],
                        axis=0,
                    )
                )
            a = jnp.concatenate(columns, axis=1)
            for c in range(2):
                acc[c, group] += contract_lanes(a, hot[c])
            return carry

        loop(groups, add, 0)
        return carry

    lax.fori_loop(0, half // SUBS, rows_step, 0)

    def give_back(group, carry):
        for c in range(2):
            for k in range(SUBS):
                base = 16 * k + 4 * c
                total = acc[c, group, base : base + 4, :] + acc[c, group, base + 8 : base + 12, :]
                ret_out[c * owners + group * SUBS + k] = total
        return carry

    loop(groups, give_back, 0)
    ret_in[me] = ret_out[me]
    spread_lists(ret_out, ret_in, 2, 3, False)

    wait_halos(1)
    smooth(1, once, dif, tr)

    cells[...] = jnp.zeros_like(cells)
    wait_lists(ret_in, 3)

    def cells_step(group, carry):
        start = pl.multiple_of(group * SUBS, SUBS)
        cell = send_cell[pl.ds(start, SUBS), :]
        low, high = cell & (LANES - 1), cell >> 7
        columns, hot = [], []
        for j in range(SUBS):
            value = ret_in[start + j] + ret_in[owners + start + j]
            mask = row_of(high, j, SUBS) == sub8
            hot.append(one_hot(low[j : j + 1]))
            parts = []
            for _ in range(3):
                part = value.astype(BF16).astype(F32)
                value = value - part
                for v in range(4):
                    parts.append(jnp.where(mask, row_of(part, v, SUBS), 0.0))
            columns.append(jnp.concatenate(parts, axis=0).astype(BF16))
        cells[...] += contract_lanes(
            jnp.concatenate(columns, axis=1), jnp.concatenate(hot, axis=1)
        )
        return carry

    loop(groups, cells_step, 0)
    for var in range(nvar):
        parts = [cells[32 * k + 8 * var : 32 * k + 8 * var + 8, :] for k in range(3)]
        flux = parts[0] + (parts[1] + parts[2])
        last = var * nlev + nlev - 1
        column = surface[var] + surface[nvar] * flux
        out[last] = column + dif[last]
        for level in range(nlev - 2, -1, -1):
            n = var * nlev + level
            column = off[n] + fac[level] * column
            out[n] = column + dif[n]

    for copy in part_copies:
        copy.wait_send()
    finish_halos(0)
    finish_halos(1)
    wait_lists(tab_in, 0)
    wait_lists(ret_in, 2)


def per_device(
    n_tile, n_sub, tracers, couple, send_cell, recv_pos, row_count, sea_mask, exch_coef, margin_area
):
    nvar, nlev = tracers.shape[1:3]
    tiles = nvar * nlev
    owners = n_tile * n_sub
    rows = recv_pos.shape[-1] // LANES
    slab = tiles // SUBS
    block = (SUBS, LANES)
    vmem = pl.BlockSpec(memory_space=pltpu.VMEM)
    hbm = pl.BlockSpec(memory_space=pltpu.HBM)
    scratch = [
        pltpu.VMEM((tiles,) + block, F32),
        pltpu.VMEM((nlev,) + block, F32),
        pltpu.VMEM((owners, LANES), jnp.int32),
        pltpu.VMEM((rows // 2, LANES), jnp.int32),
        pltpu.VMEM((nvar, rows // 2, LANES), F32),
        pltpu.SemaphoreType.DMA((7,)),
        pltpu.VMEM((tiles,) + block, F32),
        pltpu.VMEM((nlev,) + block, F32),
        pltpu.VMEM((tiles,) + block, F32),
        pltpu.VMEM((tiles,) + block, F32),
        pltpu.VMEM((owners, 4, LANES), F32),
        pltpu.VMEM((2 * owners, 4, LANES), F32),
        pltpu.VMEM((owners,) + block, F32),
        pltpu.VMEM((2, rows // 2, LANES), jnp.int32),
        pltpu.VMEM((2, rows // 2, LANES), F32),
        pltpu.VMEM((2, rows // 2, LANES), F32),
        pltpu.VMEM((2, owners // SUBS, 16 * SUBS, LANES), F32),
        pltpu.VMEM((2 * owners, 4, LANES), F32),
        pltpu.VMEM((2 * owners, 4, LANES), F32),
        pltpu.VMEM((2, 2, slab) + block, F32),
        pltpu.VMEM((2, 2, slab) + block, F32),
        pltpu.VMEM((2, 2) + block, F32),
        pltpu.VMEM((2, 2) + block, F32),
        pltpu.VMEM((96, LANES), F32),
        pltpu.SemaphoreType.DMA((4,)),
        pltpu.SemaphoreType.DMA((2, 4)),
        pltpu.SemaphoreType.DMA((2, 4)),
        pltpu.SemaphoreType.DMA((4,)),
    ]
    updated = pl.pallas_call(
        functools.partial(kernel, n_tile, n_sub, nvar, nlev),
        out_shape=jax.ShapeDtypeStruct((tiles,) + block, F32),
        in_specs=[hbm] * 4 + [pl.BlockSpec(memory_space=pltpu.SMEM)] + [hbm] * 3,
        out_specs=vmem,
        scratch_shapes=scratch,
        compiler_params=pltpu.CompilerParams(
            collective_id=0, has_side_effects=True, vmem_limit_bytes=63 * 1024 * 1024
        ),
        name="coupled_step",
    )(
        tracers.reshape((tiles,) + block),
        couple.reshape((nlev,) + block),
        send_cell.reshape(owners, LANES),
        recv_pos.reshape(rows, LANES),
        row_count,
        sea_mask.reshape(rows, LANES),
        exch_coef.reshape(nvar, rows, LANES),
        margin_area.reshape(rows, LANES),
    )
    return updated.reshape(tracers.shape)


def solution(mesh):
    placed = (
        P("comp", "member", None, "tile", "sub"),
        P("comp", "member", "tile", "sub"),
        P("comp", ("tile", "sub"), None, None),
        P("comp", ("tile", "sub"), None),
        P(("tile", "sub")),
        P(("tile", "sub"), None),
        P("member", ("tile", "sub"), None),
        P("comp", ("tile", "sub"), None),
    )
    return jax.shard_map(
        functools.partial(per_device, mesh.shape["tile"], mesh.shape["sub"]),
        mesh=mesh,
        in_specs=placed,
        out_specs=P("comp", "member", None, "tile", "sub"),
        check_vma=False,
    )
```

```python
import functools
import jax
import jax.numpy as jnp
from jax import lax
from jax.experimental import pallas as pl
from jax.experimental.pallas import tpu as pltpu
from jax.sharding import PartitionSpec as P

SMOOTH_RATE = 0.2
LANES = 128
SUBS = 8
MESH = pl.DeviceIdType.MESH
F32 = jnp.float32
BF16 = jnp.bfloat16


def lane_gather(table, index):
    return jnp.take_along_axis(table, index, axis=1, mode="promise_in_bounds")


def row_of(value, row, rows):
    return jnp.broadcast_to(value[row : row + 1], (rows, value.shape[1]))


def one_hot(low_row):
    spread = jnp.broadcast_to(low_row.astype(F32), (16, LANES)).astype(BF16)
    base = lax.broadcasted_iota(jnp.int32, (16, LANES), 0)
    one, zero = (jnp.full((16, LANES), value, BF16) for value in (1.0, 0.0))
    return jnp.concatenate(
        [
            jnp.where((base + 16 * k).astype(F32).astype(BF16) == spread, one, zero)
            for k in range(LANES // 16)
        ],
        axis=0,
    )


def contract_lanes(a, b):
    return lax.dot_general(a, b, (((1,), (1,)), ((), ())), preferred_element_type=F32)


def kernel(
    n_tile, n_sub, nvar, nlev,
    tr_hbm, couple_hbm, cell_hbm, pos, row_count, sea_hbm, coef_hbm, area,
    out,
    tr, couple, send_cell, sea, coef, load_sem,
    off, fac, once, dif, gain, hots, cell_hots, tab_out, tab_in, tabs, posb, areab, wgt, acc, ret_out, ret_in,
    row_s, row_r, col_s, col_r, cells,
    part_sem, halo_send, halo_recv, list_sem,
):
    owners = n_tile * n_sub
    groups = owners // SUBS
    tiles = nvar * nlev
    slab = tiles // SUBS
    half = pos.shape[0] // 2
    devices = 2 * owners
    comp, tile, sub = lax.axis_index("comp"), lax.axis_index("tile"), lax.axis_index("sub")
    me_owner = tile * n_sub + sub
    me = comp * owners + me_owner

    other_half = pl.multiple_of((1 - comp) * half, half)
    my_half = pl.multiple_of(comp * half, half)
    mine = pl.ds(my_half, half)
    loads = [
        pltpu.make_async_copy(source, target, load_sem.at[k])
        for k, (source, target) in enumerate(
            (
                (couple_hbm, couple),
                (tr_hbm, tr),
                (cell_hbm, send_cell),
                (pos.at[mine], posb.at[comp]),
                (area.at[mine], areab.at[comp]),
                (sea_hbm.at[mine], sea),
                (coef_hbm.at[:, mine], coef),
            )
        )
    ]
    for copy in loads:
        copy.start()

    def place(index):
        owner = index % owners
        return {"comp": index // owners, "tile": owner // n_sub, "sub": owner % n_sub}

    barrier = pltpu.get_barrier_semaphore()

    def step_on(value, step, size):
        moved = value + step
        return jnp.where(moved >= size, moved - size, moved) if step else value

    def each_other(visit):
        if devices <= 32:
            for b in range(n_tile):
                for d in range(n_sub):
                    for a in range(2):
                        if a or b or d:
                            to_comp = step_on(comp, a, 2)
                            to_tile, to_sub = step_on(tile, b, n_tile), step_on(sub, d, n_sub)
                            at = {"comp": to_comp, "tile": to_tile, "sub": to_sub}
                            owner = to_tile * n_sub + to_sub
                            visit(at, owner, to_comp * owners + owner)
        else:

            def body(step, carry):
                to = (me + step) % devices
                visit(place(to), to % owners, to)
                return carry

            lax.fori_loop(1, devices, body, 0)

    def greet(at, owner, index):
        pl.semaphore_signal(barrier, inc=1, device_id=at, device_id_type=MESH)

    each_other(greet)

    loads[0].wait()
    loads[1].wait()
    factor = None
    offset = [None] * nvar
    for level in range(nlev):
        above = couple[level]
        below = couple[level + 1] if level + 1 < nlev else jnp.zeros_like(above)
        pivot = 1.0 + above + below
        if level > 0:
            pivot = pivot - above * factor
        inverse = 1.0 / pivot
        for var in range(nvar):
            right = tr[var * nlev + level]
            if level > 0:
                right = right + above * offset[var]
            offset[var] = right * inverse
            off[var * nlev + level] = offset[var]
        factor = below * inverse
        fac[level] = factor
    surface = offset + [inverse]

    loads[2].wait()

    def make_lists(group, carry):
        start = pl.multiple_of(group * SUBS, SUBS)
        cell = send_cell[pl.ds(start, SUBS), :]
        low, high = cell & (LANES - 1), cell >> 7
        for var in range(nvar + 1):
            value = jnp.zeros((SUBS, LANES), F32)
            for a in range(SUBS):
                found = lane_gather(row_of(surface[var], a, SUBS), low)
                value = jnp.where(high == a, found, value)
            for o in range(SUBS):
                tab_out[start + o, var : var + 1, :] = value[o : o + 1]
        return carry

    def loop(count, body, carry):
        if count == 1:
            return body(0, carry)
        return lax.fori_loop(0, count, body, carry)

    loop(groups, make_lists, 0)
    tab_in[me] = tab_out[me_owner]

    pl.semaphore_wait(barrier, devices - 1)

    partner = {"comp": 1 - comp}
    part_copies = [
        pltpu.make_async_remote_copy(
            src_ref=source.at[pl.ds(other_half, half)],
            dst_ref=target.at[comp],
            send_sem=part_sem.at[2 * k],
            recv_sem=part_sem.at[2 * k + 1],
            device_id=partner,
            device_id_type=MESH,
        )
        for k, (source, target) in enumerate(((pos, posb), (area, areab)))
    ]

    def spread_lists(source, target, send, recv, by_owner):
        def visit(at, owner, index):
            pltpu.make_async_remote_copy(
                src_ref=source.at[owner if by_owner else index],
                dst_ref=target.at[me],
                send_sem=list_sem.at[send],
                recv_sem=list_sem.at[recv],
                device_id=at,
                device_id_type=MESH,
            ).start()

        each_other(visit)

    def wait_lists(target, sem):
        whole = target.at[pl.ds(0, devices - 1)]
        pltpu.make_async_copy(whole, whole, list_sem.at[sem]).wait()

    spread_lists(tab_out, tab_in, 0, 1, True)
    for copy in part_copies:
        copy.start()

    sub_iota = lax.broadcasted_iota(jnp.int32, (slab, SUBS, LANES), 1)
    lane_iota = lax.broadcasted_iota(jnp.int32, (slab, SUBS, LANES), 2)
    tile_iota = lax.broadcasted_iota(jnp.int32, (slab, SUBS, LANES), 0)

    def turn(value, shift, axis):
        return value if shift == 0 else pltpu.roll(value, shift, axis)

    links = (
        (row_s, row_r, 0, tile > 0, tile < n_tile - 1, "tile", tile),
        (col_s, col_r, 2, sub > 0, sub < n_sub - 1, "sub", sub),
    )

    def halo_copy(turn_no, link, side):
        sends, receives, base, _, _, axis, place_at = link
        return pltpu.make_async_remote_copy(
            src_ref=sends.at[turn_no, side],
            dst_ref=receives.at[turn_no, 1 - side],
            send_sem=halo_send.at[turn_no, base + side],
            recv_sem=halo_recv.at[turn_no, base + 1 - side],
            device_id={axis: place_at + (1 if side else -1)},
            device_id_type=MESH,
        )

    def send_halos(turn_no, source):
        first = jnp.zeros((slab, SUBS, LANES), F32)
        last = first
        col_first = jnp.zeros((SUBS, LANES), F32)
        col_last = col_first
        for j in range(SUBS):
            block = source[j * slab : (j + 1) * slab]
            first = jnp.where(sub_iota == j, turn(block, j, 1), first)
            last = jnp.where(sub_iota == j, turn(block, (j + 1) % SUBS, 1), last)
            here = lane_iota == tile_iota + j * slab
            shape = (slab, SUBS, LANES)
            left = jnp.broadcast_to(block[:, :, 0:1], shape)
            right = jnp.broadcast_to(block[:, :, LANES - 1 : LANES], shape)
            col_first = col_first + jnp.sum(jnp.where(here, left, 0.0), axis=0)
            col_last = col_last + jnp.sum(jnp.where(here, right, 0.0), axis=0)
        row_s[turn_no, 0] = first
        row_s[turn_no, 1] = last
        col_s[turn_no, 0] = col_first
        col_s[turn_no, 1] = col_last
        for link in links:
            for side in range(2):
                receives, there = link[1], link[3 + side]

                @pl.when(there)
                def _():
                    halo_copy(turn_no, link, side).start()

                @pl.when(jnp.logical_not(there))
                def _():
                    receives[turn_no, side] = jnp.zeros(receives.shape[2:], F32)

    def wait_halos(turn_no):
        for link in links:
            for side in range(2):

                @pl.when(link[3 + side])
                def _():
                    halo_copy(turn_no, link, 1 - side).wait_recv()

    def finish_halos(turn_no):
        for link in links:
            for side in range(2):

                @pl.when(link[3 + side])
                def _():
                    halo_copy(turn_no, link, side).wait_send()

    def smooth(turn_no, source, target, subtract):
        up_rows, down_rows = row_r[turn_no, 0], row_r[turn_no, 1]
        left_cols, right_cols = (
            jnp.broadcast_to(col_r[turn_no, side][None], (slab, SUBS, LANES)).reshape(
                slab * SUBS, LANES
            )
            for side in range(2)
        )
        for j in range(SUBS):
            block = source[j * slab : (j + 1) * slab]
            at = (tile_iota + j * slab).reshape(slab * SUBS, LANES)
            left_halo = lane_gather(left_cols, at).reshape(slab, SUBS, LANES)
            right_halo = lane_gather(right_cols, at).reshape(slab, SUBS, LANES)
            up = jnp.where(sub_iota == 0, turn(up_rows, (SUBS - j) % SUBS, 1), turn(block, 1, 1))
            down = jnp.where(
                sub_iota == SUBS - 1, turn(down_rows, SUBS - 1 - j, 1), turn(block, SUBS - 1, 1)
            )
            left = jnp.where(lane_iota == 0, left_halo, turn(block, 1, 2))
            right = jnp.where(lane_iota == LANES - 1, right_halo, turn(block, LANES - 1, 2))
            result = block + SMOOTH_RATE * ((down + up + right + left) - 4.0 * block)
            if subtract is not None:
                result = result - subtract[j * slab : (j + 1) * slab]
            target[j * slab : (j + 1) * slab] = result

    send_halos(0, tr)

    for copy in loads[3:]:
        copy.wait()
    for copy in part_copies:
        copy.wait_recv()

    def make_hots(step, carry):
        at = pl.ds(pl.multiple_of(step * SUBS, SUBS), SUBS)
        for c in range(2):
            low = posb[c, at, :] & (LANES - 1)
            for j in range(SUBS):
                hots[c, step, :, j * LANES : (j + 1) * LANES] = one_hot(low[j : j + 1])
        return carry

    lax.fori_loop(0, half // SUBS, make_hots, 0)

    def make_cell_hots(group, carry):
        start = pl.multiple_of(group * SUBS, SUBS)
        low = send_cell[pl.ds(start, SUBS), :] & (LANES - 1)
        for j in range(SUBS):
            cell_hots[group, :, j * LANES : (j + 1) * LANES] = one_hot(low[j : j + 1])
        return carry

    loop(groups, make_cell_hots, 0)

    wait_halos(0)
    smooth(0, tr, once, None)
    send_halos(1, once)

    row_number = (
        (lax.broadcasted_iota(jnp.int32, (half, LANES), 0) + my_half) * LANES
        + lax.broadcasted_iota(jnp.int32, (half, LANES), 1)
    )
    live = (row_number < row_count[0]) & (sea[...] == 1)
    for c in range(2):
        wgt[c] = jnp.where(live, areab[c], 0.0)

    wait_lists(tab_in, 1)
    sub8 = lax.broadcasted_iota(jnp.int32, (SUBS, LANES), 0)
    upper = sub8 < 4
    quarter = sub8 & 3

    def join_tables(s, carry):
        tabs[s] = jnp.concatenate([tab_in[s], tab_in[owners + s]], axis=0)
        return carry

    if groups == 1:
        for s in range(owners):
            join_tables(s, 0)
    else:
        lax.fori_loop(0, owners, join_tables, 0)
    acc[...] = jnp.zeros_like(acc)

    def rows_step(step, carry):
        start = pl.multiple_of(step * SUBS, SUBS)
        at = pl.ds(start, SUBS)
        places = [posb[c, at, :] for c in range(2)]
        weights = [wgt[c, at, :] for c in range(2)]
        coefs = [coef[v, at, :] for v in range(nvar)]
        lows, highs = [], []
        for j in range(SUBS):
            p = jnp.where(upper, row_of(places[0], j, SUBS), row_of(places[1], j, SUBS))
            lows.append(p & (LANES - 1))
            highs.append(p >> 7)

        def find(group, found):
            found = list(found)
            for k in range(SUBS):
                s = group * SUBS + k
                table = tabs[s]
                for j in range(SUBS):
                    found[j] = jnp.where(highs[j] == s, lane_gather(table, lows[j]), found[j])
            return tuple(found)

        found = loop(groups, find, tuple(jnp.zeros((SUBS, LANES), F32) for _ in range(SUBS)))
        terms, sources = [], []
        for j in range(SUBS):
            own = found[j]
            other = pltpu.roll(own, 4, 0)
            k = row_of(coefs[nvar - 1], j, SUBS)
            for v in range(nvar - 1):
                k = jnp.where(quarter == v, row_of(coefs[v], j, SUBS), k)
            w = jnp.where(upper, row_of(weights[0], j, SUBS), row_of(weights[1], j, SUBS))
            both = row_of(own + other, nvar, SUBS)
            flux = k * (other - own) / (1.0 + k * both) * w
            main = flux.astype(BF16).astype(F32)
            terms.append(jnp.concatenate([main, flux - main], axis=0).astype(BF16))
            sources.append(
                jnp.concatenate([highs[j], highs[j]], axis=0).astype(F32).astype(BF16)
            )

        def add(group, carry):
            none = jnp.zeros((16, LANES), BF16)
            columns = []
            for j in range(SUBS):
                columns.append(
                    jnp.concatenate(
                        [
                            jnp.where(
                                sources[j]
                                == jnp.full((16, LANES), group * SUBS + k, jnp.int32)
                                .astype(F32)
                                .astype(BF16),
                                terms[j],
                                none,
                            )
                            for k in range(SUBS)
                        ],
                        axis=0,
                    )
                )
            a = jnp.concatenate(columns, axis=1)
            for c in range(2):
                acc[c, group] += contract_lanes(a, hots[c, step])
            return carry

        loop(groups, add, 0)
        return carry

    lax.fori_loop(0, half // SUBS, rows_step, 0)

    def give_back(group, carry):
        for c in range(2):
            for k in range(SUBS):
                base = 16 * k + 4 * c
                total = acc[c, group, base : base + 4, :] + acc[c, group, base + 8 : base + 12, :]
                ret_out[c * owners + group * SUBS + k] = total
        return carry

    loop(groups, give_back, 0)
    ret_in[me] = ret_out[me]
    spread_lists(ret_out, ret_in, 2, 3, False)

    wait_halos(1)
    smooth(1, once, dif, tr)

    slope = surface[nvar]
    gain[nlev - 1] = slope
    for level in range(nlev - 2, -1, -1):
        slope = fac[level] * slope
        gain[level] = slope
    for var in range(nvar):
        last = var * nlev + nlev - 1
        column = surface[var]
        off[last] = column + dif[last]
        for level in range(nlev - 2, -1, -1):
            n = var * nlev + level
            column = off[n] + fac[level] * column
            off[n] = column + dif[n]

    cells[...] = jnp.zeros_like(cells)
    wait_lists(ret_in, 3)

    def cells_step(group, carry):
        start = pl.multiple_of(group * SUBS, SUBS)
        cell = send_cell[pl.ds(start, SUBS), :]
        high = cell >> 7
        columns = []
        for j in range(SUBS):
            value = ret_in[start + j] + ret_in[owners + start + j]
            mask = row_of(high, j, SUBS) == sub8
            parts = []
            for _ in range(3):
                part = value.astype(BF16).astype(F32)
                value = value - part
                for v in range(4):
                    parts.append(jnp.where(mask, row_of(part, v, SUBS), 0.0))
            columns.append(jnp.concatenate(parts, axis=0).astype(BF16))
        cells[...] += contract_lanes(
            jnp.concatenate(columns, axis=1), cell_hots[group]
        )
        return carry

    loop(groups, cells_step, 0)
    for var in range(nvar):
        parts = [cells[32 * k + 8 * var : 32 * k + 8 * var + 8, :] for k in range(3)]
        flux = parts[0] + (parts[1] + parts[2])
        for level in range(nlev):
            n = var * nlev + level
            out[n] = off[n] + gain[level] * flux

    for copy in part_copies:
        copy.wait_send()
    finish_halos(0)
    finish_halos(1)
    wait_lists(tab_in, 0)
    wait_lists(ret_in, 2)


def per_device(
    n_tile, n_sub, tracers, couple, send_cell, recv_pos, row_count, sea_mask, exch_coef, margin_area
):
    nvar, nlev = tracers.shape[1:3]
    tiles = nvar * nlev
    owners = n_tile * n_sub
    rows = recv_pos.shape[-1] // LANES
    slab = tiles // SUBS
    block = (SUBS, LANES)
    vmem = pl.BlockSpec(memory_space=pltpu.VMEM)
    hbm = pl.BlockSpec(memory_space=pltpu.HBM)
    scratch = [
        pltpu.VMEM((tiles,) + block, F32),
        pltpu.VMEM((nlev,) + block, F32),
        pltpu.VMEM((owners, LANES), jnp.int32),
        pltpu.VMEM((rows // 2, LANES), jnp.int32),
        pltpu.VMEM((nvar, rows // 2, LANES), F32),
        pltpu.SemaphoreType.DMA((7,)),
        pltpu.VMEM((tiles,) + block, F32),
        pltpu.VMEM((nlev,) + block, F32),
        pltpu.VMEM((tiles,) + block, F32),
        pltpu.VMEM((tiles,) + block, F32),
        pltpu.VMEM((nlev,) + block, F32),
        pltpu.VMEM((2, rows // 2 // SUBS, LANES, SUBS * LANES), BF16),
        pltpu.VMEM((owners // SUBS, LANES, SUBS * LANES), BF16),
        pltpu.VMEM((owners, 4, LANES), F32),
        pltpu.VMEM((2 * owners, 4, LANES), F32),
        pltpu.VMEM((owners,) + block, F32),
        pltpu.VMEM((2, rows // 2, LANES), jnp.int32),
        pltpu.VMEM((2, rows // 2, LANES), F32),
        pltpu.VMEM((2, rows // 2, LANES), F32),
        pltpu.VMEM((2, owners // SUBS, 16 * SUBS, LANES), F32),
        pltpu.VMEM((2 * owners, 4, LANES), F32),
        pltpu.VMEM((2 * owners, 4, LANES), F32),
        pltpu.VMEM((2, 2, slab) + block, F32),
        pltpu.VMEM((2, 2, slab) + block, F32),
        pltpu.VMEM((2, 2) + block, F32),
        pltpu.VMEM((2, 2) + block, F32),
        pltpu.VMEM((96, LANES), F32),
        pltpu.SemaphoreType.DMA((4,)),
        pltpu.SemaphoreType.DMA((2, 4)),
        pltpu.SemaphoreType.DMA((2, 4)),
        pltpu.SemaphoreType.DMA((4,)),
    ]
    updated = pl.pallas_call(
        functools.partial(kernel, n_tile, n_sub, nvar, nlev),
        out_shape=jax.ShapeDtypeStruct((tiles,) + block, F32),
        in_specs=[hbm] * 4 + [pl.BlockSpec(memory_space=pltpu.SMEM)] + [hbm] * 3,
        out_specs=vmem,
        scratch_shapes=scratch,
        compiler_params=pltpu.CompilerParams(
            collective_id=0, has_side_effects=True, vmem_limit_bytes=40 * 1024 * 1024
        ),
        name="coupled_step",
    )(
        pltpu.with_memory_space_constraint(tracers.reshape((tiles,) + block), pltpu.HBM),
        pltpu.with_memory_space_constraint(couple.reshape((nlev,) + block), pltpu.HBM),
        pltpu.with_memory_space_constraint(send_cell.reshape(owners, LANES), pltpu.HBM),
        pltpu.with_memory_space_constraint(recv_pos.reshape(rows, LANES), pltpu.HBM),
        row_count,
        pltpu.with_memory_space_constraint(sea_mask.reshape(rows, LANES), pltpu.HBM),
        pltpu.with_memory_space_constraint(exch_coef.reshape(nvar, rows, LANES), pltpu.HBM),
        pltpu.with_memory_space_constraint(margin_area.reshape(rows, LANES), pltpu.HBM),
    )
    return updated.reshape(tracers.shape)


def solution(mesh):
    placed = (
        P("comp", "member", None, "tile", "sub"),
        P("comp", "member", "tile", "sub"),
        P("comp", ("tile", "sub"), None, None),
        P("comp", ("tile", "sub"), None),
        P(("tile", "sub")),
        P(("tile", "sub"), None),
        P("member", ("tile", "sub"), None),
        P("comp", ("tile", "sub"), None),
    )
    return jax.shard_map(
        functools.partial(per_device, mesh.shape["tile"], mesh.shape["sub"]),
        mesh=mesh,
        in_specs=placed,
        out_specs=P("comp", "member", None, "tile", "sub"),
        check_vma=False,
    )
```

```python
import functools
import jax
import jax.numpy as jnp
from jax import lax
from jax.experimental import pallas as pl
from jax.experimental.pallas import tpu as pltpu
from jax.sharding import PartitionSpec as P

SMOOTH_RATE = 0.2
LANES = 128
SUBS = 8
MESH = pl.DeviceIdType.MESH
F32 = jnp.float32
BF16 = jnp.bfloat16


def lane_gather(table, index):
    return jnp.take_along_axis(table, index, axis=1, mode="promise_in_bounds")


def row_of(value, row, rows):
    return jnp.broadcast_to(value[row : row + 1], (rows, value.shape[1]))


def one_hot(low_row):
    spread = jnp.broadcast_to(low_row.astype(F32), (16, LANES)).astype(BF16)
    base = lax.broadcasted_iota(jnp.int32, (16, LANES), 0)
    one, zero = (jnp.full((16, LANES), value, BF16) for value in (1.0, 0.0))
    return jnp.concatenate(
        [
            jnp.where((base + 16 * k).astype(F32).astype(BF16) == spread, one, zero)
            for k in range(LANES // 16)
        ],
        axis=0,
    )


def contract_lanes(a, b):
    return lax.dot_general(a, b, (((1,), (1,)), ((), ())), preferred_element_type=F32)


def kernel(
    n_tile, n_sub, nvar, nlev,
    tr_hbm, couple_hbm, cell_hbm, pos, row_count, sea_hbm, coef_hbm, area,
    out,
    tr, couple, send_cell, sea, coef, load_sem,
    off, fac, once, dif, gain, hots, cell_hots, tab_out, tab_in, tabs, posb, areab, wgt, acc, ret_out, ret_in,
    row_s, row_r, col_s, col_r, cells,
    part_sem, halo_send, halo_recv, list_sem,
):
    owners = n_tile * n_sub
    groups = owners // SUBS
    tiles = nvar * nlev
    slab = tiles // SUBS
    half = pos.shape[0] // 2
    devices = 2 * owners
    comp, tile, sub = lax.axis_index("comp"), lax.axis_index("tile"), lax.axis_index("sub")
    me_owner = tile * n_sub + sub
    me = comp * owners + me_owner

    other_half = pl.multiple_of((1 - comp) * half, half)
    my_half = pl.multiple_of(comp * half, half)
    mine = pl.ds(my_half, half)
    loads = [
        pltpu.make_async_copy(source, target, load_sem.at[k])
        for k, (source, target) in enumerate(
            (
                (couple_hbm, couple),
                (tr_hbm, tr),
                (cell_hbm, send_cell),
                (pos.at[mine], posb.at[comp]),
                (area.at[mine], areab.at[comp]),
                (sea_hbm.at[mine], sea),
                (coef_hbm.at[:, mine], coef),
            )
        )
    ]
    def place(index):
        owner = index % owners
        return {"comp": index // owners, "tile": owner // n_sub, "sub": owner % n_sub}

    barrier = pltpu.get_barrier_semaphore()

    def each_other(visit):
        if devices <= 32 and n_tile & (n_tile - 1) == 0 and n_sub & (n_sub - 1) == 0:
            for b in range(n_tile - 1, -1, -1):
                for d in range(n_sub - 1, -1, -1):
                    for a in range(2):
                        if a or b or d:
                            to_comp, to_tile, to_sub = comp ^ a, tile ^ b, sub ^ d
                            at = {"comp": to_comp, "tile": to_tile, "sub": to_sub}
                            owner = to_tile * n_sub + to_sub
                            visit(at, owner, to_comp * owners + owner)
        else:

            def body(step, carry):
                to = (me + step) % devices
                visit(place(to), to % owners, to)
                return carry

            lax.fori_loop(1, devices, body, 0)

    def greet(at, owner, index):
        pl.semaphore_signal(barrier, inc=1, device_id=at, device_id_type=MESH)

    each_other(greet)
    for copy in loads:
        copy.start()

    loads[0].wait()
    loads[1].wait()
    factor = None
    offset = [None] * nvar
    for level in range(nlev):
        above = couple[level]
        below = couple[level + 1] if level + 1 < nlev else jnp.zeros_like(above)
        pivot = 1.0 + above + below
        if level > 0:
            pivot = pivot - above * factor
        inverse = 1.0 / pivot
        for var in range(nvar):
            right = tr[var * nlev + level]
            if level > 0:
                right = right + above * offset[var]
            offset[var] = right * inverse
            off[var * nlev + level] = offset[var]
        factor = below * inverse
        fac[level] = factor
    surface = offset + [inverse]

    loads[2].wait()

    def make_lists(group, carry):
        start = pl.multiple_of(group * SUBS, SUBS)
        cell = send_cell[pl.ds(start, SUBS), :]
        low, high = cell & (LANES - 1), cell >> 7
        for var in range(nvar + 1):
            value = jnp.zeros((SUBS, LANES), F32)
            for a in range(SUBS):
                found = lane_gather(row_of(surface[var], a, SUBS), low)
                value = jnp.where(high == a, found, value)
            for o in range(SUBS):
                tab_out[start + o, var : var + 1, :] = value[o : o + 1]
        return carry

    def loop(count, body, carry):
        if count == 1:
            return body(0, carry)
        return lax.fori_loop(0, count, body, carry)

    loop(groups, make_lists, 0)
    tab_in[me] = tab_out[me_owner]

    pl.semaphore_wait(barrier, devices - 1)

    partner = {"comp": 1 - comp}
    part_copies = [
        pltpu.make_async_remote_copy(
            src_ref=source.at[pl.ds(other_half, half)],
            dst_ref=target.at[comp],
            send_sem=part_sem.at[2 * k],
            recv_sem=part_sem.at[2 * k + 1],
            device_id=partner,
            device_id_type=MESH,
        )
        for k, (source, target) in enumerate(((pos, posb), (area, areab)))
    ]

    def spread_lists(source, target, send, recv, by_owner):
        def visit(at, owner, index):
            pltpu.make_async_remote_copy(
                src_ref=source.at[owner if by_owner else index],
                dst_ref=target.at[me],
                send_sem=list_sem.at[send],
                recv_sem=list_sem.at[recv],
                device_id=at,
                device_id_type=MESH,
            ).start()

        each_other(visit)

    def wait_lists(target, sem):
        whole = target.at[pl.ds(0, devices - 1)]
        pltpu.make_async_copy(whole, whole, list_sem.at[sem]).wait()

    spread_lists(tab_out, tab_in, 0, 1, True)
    for copy in part_copies:
        copy.start()

    sub_iota = lax.broadcasted_iota(jnp.int32, (slab, SUBS, LANES), 1)
    lane_iota = lax.broadcasted_iota(jnp.int32, (slab, SUBS, LANES), 2)
    tile_iota = lax.broadcasted_iota(jnp.int32, (slab, SUBS, LANES), 0)

    def turn(value, shift, axis):
        return value if shift == 0 else pltpu.roll(value, shift, axis)

    links = (
        (row_s, row_r, 0, tile > 0, tile < n_tile - 1, "tile", tile),
        (col_s, col_r, 2, sub > 0, sub < n_sub - 1, "sub", sub),
    )

    def halo_copy(turn_no, link, side):
        sends, receives, base, _, _, axis, place_at = link
        return pltpu.make_async_remote_copy(
            src_ref=sends.at[turn_no, side],
            dst_ref=receives.at[turn_no, 1 - side],
            send_sem=halo_send.at[turn_no, base + side],
            recv_sem=halo_recv.at[turn_no, base + 1 - side],
            device_id={axis: place_at + (1 if side else -1)},
            device_id_type=MESH,
        )

    def send_halos(turn_no, source):
        first = jnp.zeros((slab, SUBS, LANES), F32)
        last = first
        col_first = jnp.zeros((SUBS, LANES), F32)
        col_last = col_first
        for j in range(SUBS):
            block = source[j * slab : (j + 1) * slab]
            first = jnp.where(sub_iota == j, turn(block, j, 1), first)
            last = jnp.where(sub_iota == j, turn(block, (j + 1) % SUBS, 1), last)
            here = lane_iota == tile_iota + j * slab
            shape = (slab, SUBS, LANES)
            left = jnp.broadcast_to(block[:, :, 0:1], shape)
            right = jnp.broadcast_to(block[:, :, LANES - 1 : LANES], shape)
            col_first = col_first + jnp.sum(jnp.where(here, left, 0.0), axis=0)
            col_last = col_last + jnp.sum(jnp.where(here, right, 0.0), axis=0)
        row_s[turn_no, 0] = first
        row_s[turn_no, 1] = last
        col_s[turn_no, 0] = col_first
        col_s[turn_no, 1] = col_last
        for link in links:
            for side in range(2):
                receives, there = link[1], link[3 + side]

                @pl.when(there)
                def _():
                    halo_copy(turn_no, link, side).start()

                @pl.when(jnp.logical_not(there))
                def _():
                    receives[turn_no, side] = jnp.zeros(receives.shape[2:], F32)

    def wait_halos(turn_no):
        for link in links:
            for side in range(2):

                @pl.when(link[3 + side])
                def _():
                    halo_copy(turn_no, link, 1 - side).wait_recv()

    def finish_halos(turn_no):
        for link in links:
            for side in range(2):

                @pl.when(link[3 + side])
                def _():
                    halo_copy(turn_no, link, side).wait_send()

    def smooth(turn_no, source, target, subtract):
        up_rows, down_rows = row_r[turn_no, 0], row_r[turn_no, 1]
        left_cols, right_cols = (
            jnp.broadcast_to(col_r[turn_no, side][None], (slab, SUBS, LANES)).reshape(
                slab * SUBS, LANES
            )
            for side in range(2)
        )
        for j in range(SUBS):
            block = source[j * slab : (j + 1) * slab]
            at = (tile_iota + j * slab).reshape(slab * SUBS, LANES)
            left_halo = lane_gather(left_cols, at).reshape(slab, SUBS, LANES)
            right_halo = lane_gather(right_cols, at).reshape(slab, SUBS, LANES)
            up = jnp.where(sub_iota == 0, turn(up_rows, (SUBS - j) % SUBS, 1), turn(block, 1, 1))
            down = jnp.where(
                sub_iota == SUBS - 1, turn(down_rows, SUBS - 1 - j, 1), turn(block, SUBS - 1, 1)
            )
            left = jnp.where(lane_iota == 0, left_halo, turn(block, 1, 2))
            right = jnp.where(lane_iota == LANES - 1, right_halo, turn(block, LANES - 1, 2))
            result = block + SMOOTH_RATE * ((down + up + right + left) - 4.0 * block)
            if subtract is not None:
                result = result - subtract[j * slab : (j + 1) * slab]
            target[j * slab : (j + 1) * slab] = result

    send_halos(0, tr)

    for copy in loads[3:]:
        copy.wait()
    for copy in part_copies:
        copy.wait_recv()

    def make_hots(step, carry):
        at = pl.ds(pl.multiple_of(step * SUBS, SUBS), SUBS)
        for c in range(2):
            low = posb[c, at, :] & (LANES - 1)
            for j in range(SUBS):
                hots[c, step, :, j * LANES : (j + 1) * LANES] = one_hot(low[j : j + 1])
        return carry

    lax.fori_loop(0, half // SUBS, make_hots, 0)

    def make_cell_hots(group, carry):
        start = pl.multiple_of(group * SUBS, SUBS)
        low = send_cell[pl.ds(start, SUBS), :] & (LANES - 1)
        for j in range(SUBS):
            cell_hots[group, :, j * LANES : (j + 1) * LANES] = one_hot(low[j : j + 1])
        return carry

    loop(groups, make_cell_hots, 0)

    wait_halos(0)
    smooth(0, tr, once, None)
    send_halos(1, once)

    row_number = (
        (lax.broadcasted_iota(jnp.int32, (half, LANES), 0) + my_half) * LANES
        + lax.broadcasted_iota(jnp.int32, (half, LANES), 1)
    )
    live = (row_number < row_count[0]) & (sea[...] == 1)
    for c in range(2):
        wgt[c] = jnp.where(live, areab[c], 0.0)

    wait_lists(tab_in, 1)
    sub8 = lax.broadcasted_iota(jnp.int32, (SUBS, LANES), 0)
    upper = sub8 < 4
    quarter = sub8 & 3

    def join_tables(s, carry):
        tabs[s] = jnp.concatenate([tab_in[s], tab_in[owners + s]], axis=0)
        return carry

    if groups == 1:
        for s in range(owners):
            join_tables(s, 0)
    else:
        lax.fori_loop(0, owners, join_tables, 0)
    acc[...] = jnp.zeros_like(acc)

    def rows_step(step, carry):
        start = pl.multiple_of(step * SUBS, SUBS)
        at = pl.ds(start, SUBS)
        places = [posb[c, at, :] for c in range(2)]
        weights = [wgt[c, at, :] for c in range(2)]
        coefs = [coef[v, at, :] for v in range(nvar)]
        lows, highs = [], []
        for j in range(SUBS):
            p = jnp.where(upper, row_of(places[0], j, SUBS), row_of(places[1], j, SUBS))
            lows.append(p & (LANES - 1))
            highs.append(p >> 7)

        def find(group, found):
            found = list(found)
            for k in range(SUBS):
                s = group * SUBS + k
                table = tabs[s]
                for j in range(SUBS):
                    found[j] = jnp.where(highs[j] == s, lane_gather(table, lows[j]), found[j])
            return tuple(found)

        found = loop(groups, find, tuple(jnp.zeros((SUBS, LANES), F32) for _ in range(SUBS)))
        terms, sources = [], []
        for j in range(SUBS):
            own = found[j]
            other = pltpu.roll(own, 4, 0)
            k = row_of(coefs[nvar - 1], j, SUBS)
            for v in range(nvar - 1):
                k = jnp.where(quarter == v, row_of(coefs[v], j, SUBS), k)
            w = jnp.where(upper, row_of(weights[0], j, SUBS), row_of(weights[1], j, SUBS))
            both = row_of(own + other, nvar, SUBS)
            flux = k * (other - own) / (1.0 + k * both) * w
            main = flux.astype(BF16).astype(F32)
            terms.append(jnp.concatenate([main, flux - main], axis=0).astype(BF16))
            sources.append(
                jnp.concatenate([highs[j], highs[j]], axis=0).astype(F32).astype(BF16)
            )

        def add(group, carry):
            none = jnp.zeros((16, LANES), BF16)
            columns = []
            for j in range(SUBS):
                columns.append(
                    jnp.concatenate(
                        [
                            jnp.where(
                                sources[j]
                                == jnp.full((16, LANES), group * SUBS + k, jnp.int32)
                                .astype(F32)
                                .astype(BF16),
                                terms[j],
                                none,
                            )
                            for k in range(SUBS)
                        ],
                        axis=0,
                    )
                )
            a = jnp.concatenate(columns, axis=1)
            for c in range(2):
                acc[c, group] += contract_lanes(a, hots[c, step])
            return carry

        loop(groups, add, 0)
        return carry

    lax.fori_loop(0, half // SUBS, rows_step, 0, unroll=4)

    def give_back(group, carry):
        for c in range(2):
            for k in range(SUBS):
                base = 16 * k + 4 * c
                total = acc[c, group, base : base + 4, :] + acc[c, group, base + 8 : base + 12, :]
                ret_out[c * owners + group * SUBS + k] = total
        return carry

    loop(groups, give_back, 0)
    ret_in[me] = ret_out[me]
    spread_lists(ret_out, ret_in, 2, 3, False)

    wait_halos(1)
    smooth(1, once, dif, tr)

    slope = surface[nvar]
    gain[nlev - 1] = slope
    for level in range(nlev - 2, -1, -1):
        slope = fac[level] * slope
        gain[level] = slope
    for var in range(nvar):
        last = var * nlev + nlev - 1
        column = surface[var]
        off[last] = column + dif[last]
        for level in range(nlev - 2, -1, -1):
            n = var * nlev + level
            column = off[n] + fac[level] * column
            off[n] = column + dif[n]

    cells[...] = jnp.zeros_like(cells)
    wait_lists(ret_in, 3)

    def cells_step(group, carry):
        start = pl.multiple_of(group * SUBS, SUBS)
        cell = send_cell[pl.ds(start, SUBS), :]
        high = cell >> 7
        columns = []
        for j in range(SUBS):
            value = ret_in[start + j] + ret_in[owners + start + j]
            mask = row_of(high, j, SUBS) == sub8
            parts = []
            for _ in range(3):
                part = value.astype(BF16).astype(F32)
                value = value - part
                for v in range(4):
                    parts.append(jnp.where(mask, row_of(part, v, SUBS), 0.0))
            columns.append(jnp.concatenate(parts, axis=0).astype(BF16))
        cells[...] += contract_lanes(
            jnp.concatenate(columns, axis=1), cell_hots[group]
        )
        return carry

    loop(groups, cells_step, 0)
    for var in range(nvar):
        parts = [cells[32 * k + 8 * var : 32 * k + 8 * var + 8, :] for k in range(3)]
        flux = parts[0] + (parts[1] + parts[2])
        for level in range(nlev):
            n = var * nlev + level
            out[n] = off[n] + gain[level] * flux

    for copy in part_copies:
        copy.wait_send()
    finish_halos(0)
    finish_halos(1)
    wait_lists(tab_in, 0)
    wait_lists(ret_in, 2)


def per_device(
    n_tile, n_sub, tracers, couple, send_cell, recv_pos, row_count, sea_mask, exch_coef, margin_area
):
    nvar, nlev = tracers.shape[1:3]
    tiles = nvar * nlev
    owners = n_tile * n_sub
    rows = recv_pos.shape[-1] // LANES
    slab = tiles // SUBS
    block = (SUBS, LANES)
    vmem = pl.BlockSpec(memory_space=pltpu.VMEM)
    hbm = pl.BlockSpec(memory_space=pltpu.HBM)
    scratch = [
        pltpu.VMEM((tiles,) + block, F32),
        pltpu.VMEM((nlev,) + block, F32),
        pltpu.VMEM((owners, LANES), jnp.int32),
        pltpu.VMEM((rows // 2, LANES), jnp.int32),
        pltpu.VMEM((nvar, rows // 2, LANES), F32),
        pltpu.SemaphoreType.DMA((7,)),
        pltpu.VMEM((tiles,) + block, F32),
        pltpu.VMEM((nlev,) + block, F32),
        pltpu.VMEM((tiles,) + block, F32),
        pltpu.VMEM((tiles,) + block, F32),
        pltpu.VMEM((nlev,) + block, F32),
        pltpu.VMEM((2, rows // 2 // SUBS, LANES, SUBS * LANES), BF16),
        pltpu.VMEM((owners // SUBS, LANES, SUBS * LANES), BF16),
        pltpu.VMEM((owners, 4, LANES), F32),
        pltpu.VMEM((2 * owners, 4, LANES), F32),
        pltpu.VMEM((owners,) + block, F32),
        pltpu.VMEM((2, rows // 2, LANES), jnp.int32),
        pltpu.VMEM((2, rows // 2, LANES), F32),
        pltpu.VMEM((2, rows // 2, LANES), F32),
        pltpu.VMEM((2, owners // SUBS, 16 * SUBS, LANES), F32),
        pltpu.VMEM((2 * owners, 4, LANES), F32),
        pltpu.VMEM((2 * owners, 4, LANES), F32),
        pltpu.VMEM((2, 2, slab) + block, F32),
        pltpu.VMEM((2, 2, slab) + block, F32),
        pltpu.VMEM((2, 2) + block, F32),
        pltpu.VMEM((2, 2) + block, F32),
        pltpu.VMEM((96, LANES), F32),
        pltpu.SemaphoreType.DMA((4,)),
        pltpu.SemaphoreType.DMA((2, 4)),
        pltpu.SemaphoreType.DMA((2, 4)),
        pltpu.SemaphoreType.DMA((4,)),
    ]
    updated = pl.pallas_call(
        functools.partial(kernel, n_tile, n_sub, nvar, nlev),
        out_shape=jax.ShapeDtypeStruct((tiles,) + block, F32),
        in_specs=[hbm] * 4 + [pl.BlockSpec(memory_space=pltpu.SMEM)] + [hbm] * 3,
        out_specs=vmem,
        scratch_shapes=scratch,
        compiler_params=pltpu.CompilerParams(
            collective_id=0, has_side_effects=True, vmem_limit_bytes=40 * 1024 * 1024
        ),
        name="coupled_step",
    )(
        pltpu.with_memory_space_constraint(tracers.reshape((tiles,) + block), pltpu.HBM),
        pltpu.with_memory_space_constraint(couple.reshape((nlev,) + block), pltpu.HBM),
        pltpu.with_memory_space_constraint(send_cell.reshape(owners, LANES), pltpu.HBM),
        pltpu.with_memory_space_constraint(recv_pos.reshape(rows, LANES), pltpu.HBM),
        row_count,
        pltpu.with_memory_space_constraint(sea_mask.reshape(rows, LANES), pltpu.HBM),
        pltpu.with_memory_space_constraint(exch_coef.reshape(nvar, rows, LANES), pltpu.HBM),
        pltpu.with_memory_space_constraint(margin_area.reshape(rows, LANES), pltpu.HBM),
    )
    return updated.reshape(tracers.shape)


def solution(mesh):
    placed = (
        P("comp", "member", None, "tile", "sub"),
        P("comp", "member", "tile", "sub"),
        P("comp", ("tile", "sub"), None, None),
        P("comp", ("tile", "sub"), None),
        P(("tile", "sub")),
        P(("tile", "sub"), None),
        P("member", ("tile", "sub"), None),
        P("comp", ("tile", "sub"), None),
    )
    return jax.shard_map(
        functools.partial(per_device, mesh.shape["tile"], mesh.shape["sub"]),
        mesh=mesh,
        in_specs=placed,
        out_specs=P("comp", "member", None, "tile", "sub"),
        check_vma=False,
    )
```

```python
import functools
import jax
import jax.numpy as jnp
from jax import lax
from jax.experimental import pallas as pl
from jax.experimental.pallas import tpu as pltpu
from jax.sharding import PartitionSpec as P

SMOOTH_RATE = 0.2
LANES = 128
SUBS = 8
MESH = pl.DeviceIdType.MESH
F32 = jnp.float32
BF16 = jnp.bfloat16


def lane_gather(table, index):
    return jnp.take_along_axis(table, index, axis=1, mode="promise_in_bounds")


def row_of(value, row, rows):
    return jnp.broadcast_to(value[row : row + 1], (rows, value.shape[1]))


def one_hot(low_row):
    spread = jnp.broadcast_to(low_row.astype(F32), (16, LANES)).astype(BF16)
    base = lax.broadcasted_iota(jnp.int32, (16, LANES), 0)
    one, zero = (jnp.full((16, LANES), value, BF16) for value in (1.0, 0.0))
    return jnp.concatenate(
        [
            jnp.where((base + 16 * k).astype(F32).astype(BF16) == spread, one, zero)
            for k in range(LANES // 16)
        ],
        axis=0,
    )


def contract_lanes(a, b):
    return lax.dot_general(a, b, (((1,), (1,)), ((), ())), preferred_element_type=F32)


def kernel(
    n_tile, n_sub, nvar, nlev,
    tr_hbm, couple_hbm, cell_hbm, pos, row_count, sea_hbm, coef_hbm, area,
    out,
    tr, couple, send_cell, sea, coef, load_sem,
    off, fac, once, dif, gain, hots, cell_hots, tab_out, tab_in, tabs, posb, areab, wgt, acc, ret_out, ret_in,
    row_s, row_r, col_s, col_r, cells,
    part_sem, halo_send, halo_recv, list_sem,
):
    owners = n_tile * n_sub
    groups = owners // SUBS
    tiles = nvar * nlev
    slab = tiles // SUBS
    half = pos.shape[0] // 2
    devices = 2 * owners
    comp, tile, sub = lax.axis_index("comp"), lax.axis_index("tile"), lax.axis_index("sub")
    me_owner = tile * n_sub + sub
    me = comp * owners + me_owner

    other_half = pl.multiple_of((1 - comp) * half, half)
    my_half = pl.multiple_of(comp * half, half)
    mine = pl.ds(my_half, half)
    loads = [
        pltpu.make_async_copy(source, target, load_sem.at[k])
        for k, (source, target) in enumerate(
            (
                (couple_hbm, couple),
                (tr_hbm, tr),
                (cell_hbm, send_cell),
                (pos.at[mine], posb.at[comp]),
                (area.at[mine], areab.at[comp]),
                (sea_hbm.at[mine], sea),
                (coef_hbm.at[:, mine], coef),
            )
        )
    ]
    def place(index):
        owner = index % owners
        return {"comp": index // owners, "tile": owner // n_sub, "sub": owner % n_sub}

    barrier = pltpu.get_barrier_semaphore()

    def each_other(visit):
        if devices <= 32 and n_tile & (n_tile - 1) == 0 and n_sub & (n_sub - 1) == 0:
            for b in range(n_tile - 1, -1, -1):
                for d in range(n_sub - 1, -1, -1):
                    for a in range(2):
                        if a or b or d:
                            to_comp, to_tile, to_sub = comp ^ a, tile ^ b, sub ^ d
                            at = {"comp": to_comp, "tile": to_tile, "sub": to_sub}
                            owner = to_tile * n_sub + to_sub
                            visit(at, owner, to_comp * owners + owner)
        else:

            def body(step, carry):
                to = (me + step) % devices
                visit(place(to), to % owners, to)
                return carry

            lax.fori_loop(1, devices, body, 0)

    def greet(at, owner, index):
        pl.semaphore_signal(barrier, inc=1, device_id=at, device_id_type=MESH)

    each_other(greet)
    for copy in loads:
        copy.start()

    loads[0].wait()
    loads[1].wait()
    factor = None
    offset = [None] * nvar
    for level in range(nlev):
        above = couple[level]
        below = couple[level + 1] if level + 1 < nlev else jnp.zeros_like(above)
        pivot = 1.0 + above + below
        if level > 0:
            pivot = pivot - above * factor
        inverse = 1.0 / pivot
        for var in range(nvar):
            right = tr[var * nlev + level]
            if level > 0:
                right = right + above * offset[var]
            offset[var] = right * inverse
            off[var * nlev + level] = offset[var]
        factor = below * inverse
        fac[level] = factor
    surface = offset + [inverse]

    loads[2].wait()

    def make_lists(group, carry):
        start = pl.multiple_of(group * SUBS, SUBS)
        cell = send_cell[pl.ds(start, SUBS), :]
        low, high = cell & (LANES - 1), cell >> 7
        for var in range(nvar + 1):
            value = jnp.zeros((SUBS, LANES), F32)
            for a in range(SUBS):
                found = lane_gather(row_of(surface[var], a, SUBS), low)
                value = jnp.where(high == a, found, value)
            for o in range(SUBS):
                tab_out[start + o, var : var + 1, :] = value[o : o + 1]
        return carry

    def loop(count, body, carry):
        if count == 1:
            return body(0, carry)
        return lax.fori_loop(0, count, body, carry)

    loop(groups, make_lists, 0)
    tab_in[me] = tab_out[me_owner]

    pl.semaphore_wait(barrier, devices - 1)

    partner = {"comp": 1 - comp}
    part_copies = [
        pltpu.make_async_remote_copy(
            src_ref=source.at[pl.ds(other_half, half)],
            dst_ref=target.at[comp],
            send_sem=part_sem.at[2 * k],
            recv_sem=part_sem.at[2 * k + 1],
            device_id=partner,
            device_id_type=MESH,
        )
        for k, (source, target) in enumerate(((pos, posb), (area, areab)))
    ]

    def spread_lists(source, target, send, recv, by_owner):
        def visit(at, owner, index):
            pltpu.make_async_remote_copy(
                src_ref=source.at[owner if by_owner else index],
                dst_ref=target.at[me],
                send_sem=list_sem.at[send],
                recv_sem=list_sem.at[recv],
                device_id=at,
                device_id_type=MESH,
            ).start()

        each_other(visit)

    def wait_lists(target, sem):
        whole = target.at[pl.ds(0, devices - 1)]
        pltpu.make_async_copy(whole, whole, list_sem.at[sem]).wait()

    spread_lists(tab_out, tab_in, 0, 1, True)
    for copy in part_copies:
        copy.start()

    sub_iota = lax.broadcasted_iota(jnp.int32, (slab, SUBS, LANES), 1)
    lane_iota = lax.broadcasted_iota(jnp.int32, (slab, SUBS, LANES), 2)
    tile_iota = lax.broadcasted_iota(jnp.int32, (slab, SUBS, LANES), 0)

    def turn(value, shift, axis):
        return value if shift == 0 else pltpu.roll(value, shift, axis)

    links = (
        (row_s, row_r, 0, tile > 0, tile < n_tile - 1, "tile", tile),
        (col_s, col_r, 2, sub > 0, sub < n_sub - 1, "sub", sub),
    )

    def halo_copy(turn_no, link, side):
        sends, receives, base, _, _, axis, place_at = link
        return pltpu.make_async_remote_copy(
            src_ref=sends.at[turn_no, side],
            dst_ref=receives.at[turn_no, 1 - side],
            send_sem=halo_send.at[turn_no, base + side],
            recv_sem=halo_recv.at[turn_no, base + 1 - side],
            device_id={axis: place_at + (1 if side else -1)},
            device_id_type=MESH,
        )

    def send_halos(turn_no, source):
        first = jnp.zeros((slab, SUBS, LANES), F32)
        last = first
        col_first = jnp.zeros((SUBS, LANES), F32)
        col_last = col_first
        for j in range(SUBS):
            block = source[j * slab : (j + 1) * slab]
            first = jnp.where(sub_iota == j, turn(block, j, 1), first)
            last = jnp.where(sub_iota == j, turn(block, (j + 1) % SUBS, 1), last)
            here = lane_iota == tile_iota + j * slab
            shape = (slab, SUBS, LANES)
            left = jnp.broadcast_to(block[:, :, 0:1], shape)
            right = jnp.broadcast_to(block[:, :, LANES - 1 : LANES], shape)
            col_first = col_first + jnp.sum(jnp.where(here, left, 0.0), axis=0)
            col_last = col_last + jnp.sum(jnp.where(here, right, 0.0), axis=0)
        row_s[turn_no, 0] = first
        row_s[turn_no, 1] = last
        col_s[turn_no, 0] = col_first
        col_s[turn_no, 1] = col_last
        for link in links:
            for side in range(2):
                receives, there = link[1], link[3 + side]

                @pl.when(there)
                def _():
                    halo_copy(turn_no, link, side).start()

                @pl.when(jnp.logical_not(there))
                def _():
                    receives[turn_no, side] = jnp.zeros(receives.shape[2:], F32)

    def wait_halos(turn_no):
        for link in links:
            for side in range(2):

                @pl.when(link[3 + side])
                def _():
                    halo_copy(turn_no, link, 1 - side).wait_recv()

    def finish_halos(turn_no):
        for link in links:
            for side in range(2):

                @pl.when(link[3 + side])
                def _():
                    halo_copy(turn_no, link, side).wait_send()

    def smooth(turn_no, source, target, subtract):
        up_rows, down_rows = row_r[turn_no, 0], row_r[turn_no, 1]
        left_cols, right_cols = (
            jnp.broadcast_to(col_r[turn_no, side][None], (slab, SUBS, LANES)).reshape(
                slab * SUBS, LANES
            )
            for side in range(2)
        )
        for j in range(SUBS):
            block = source[j * slab : (j + 1) * slab]
            at = (tile_iota + j * slab).reshape(slab * SUBS, LANES)
            left_halo = lane_gather(left_cols, at).reshape(slab, SUBS, LANES)
            right_halo = lane_gather(right_cols, at).reshape(slab, SUBS, LANES)
            up = jnp.where(sub_iota == 0, turn(up_rows, (SUBS - j) % SUBS, 1), turn(block, 1, 1))
            down = jnp.where(
                sub_iota == SUBS - 1, turn(down_rows, SUBS - 1 - j, 1), turn(block, SUBS - 1, 1)
            )
            left = jnp.where(lane_iota == 0, left_halo, turn(block, 1, 2))
            right = jnp.where(lane_iota == LANES - 1, right_halo, turn(block, LANES - 1, 2))
            result = block + SMOOTH_RATE * ((down + up + right + left) - 4.0 * block)
            if subtract is not None:
                result = result - subtract[j * slab : (j + 1) * slab]
            target[j * slab : (j + 1) * slab] = result

    send_halos(0, tr)

    for copy in loads[3:]:
        copy.wait()
    for copy in part_copies:
        copy.wait_recv()

    def make_hots(step, carry):
        at = pl.ds(pl.multiple_of(step * SUBS, SUBS), SUBS)
        for c in range(2):
            low = posb[c, at, :] & (LANES - 1)
            for j in range(SUBS):
                hots[c, step, :, j * LANES : (j + 1) * LANES] = one_hot(low[j : j + 1])
        return carry

    lax.fori_loop(0, half // SUBS, make_hots, 0)

    def make_cell_hots(group, carry):
        start = pl.multiple_of(group * SUBS, SUBS)
        low = send_cell[pl.ds(start, SUBS), :] & (LANES - 1)
        for j in range(SUBS):
            cell_hots[group, :, j * LANES : (j + 1) * LANES] = one_hot(low[j : j + 1])
        return carry

    loop(groups, make_cell_hots, 0)

    wait_halos(0)
    smooth(0, tr, once, None)
    send_halos(1, once)

    row_number = (
        (lax.broadcasted_iota(jnp.int32, (half, LANES), 0) + my_half) * LANES
        + lax.broadcasted_iota(jnp.int32, (half, LANES), 1)
    )
    live = (row_number < row_count[0]) & (sea[...] == 1)
    for c in range(2):
        wgt[c] = jnp.where(live, areab[c], 0.0)

    wait_lists(tab_in, 1)
    sub8 = lax.broadcasted_iota(jnp.int32, (SUBS, LANES), 0)
    upper = sub8 < 4
    quarter = sub8 & 3

    def join_tables(s, carry):
        tabs[s] = jnp.concatenate([tab_in[s], tab_in[owners + s]], axis=0)
        return carry

    if groups == 1:
        for s in range(owners):
            join_tables(s, 0)
    else:
        lax.fori_loop(0, owners, join_tables, 0)
    acc[...] = jnp.zeros_like(acc)

    def rows_step(step, carry):
        start = pl.multiple_of(step * SUBS, SUBS)
        at = pl.ds(start, SUBS)
        places = [posb[c, at, :] for c in range(2)]
        weights = [wgt[c, at, :] for c in range(2)]
        coefs = [coef[v, at, :] for v in range(nvar)]
        lows, highs = [], []
        for j in range(SUBS):
            p = jnp.where(upper, row_of(places[0], j, SUBS), row_of(places[1], j, SUBS))
            lows.append(p & (LANES - 1))
            highs.append(p >> 7)

        def find(group, found):
            found = list(found)
            for k in range(SUBS):
                s = group * SUBS + k
                table = tabs[s]
                for j in range(SUBS):
                    found[j] = jnp.where(highs[j] == s, lane_gather(table, lows[j]), found[j])
            return tuple(found)

        found = loop(groups, find, tuple(jnp.zeros((SUBS, LANES), F32) for _ in range(SUBS)))
        terms, sources = [], []
        for j in range(SUBS):
            own = found[j]
            other = pltpu.roll(own, 4, 0)
            k = row_of(coefs[nvar - 1], j, SUBS)
            for v in range(nvar - 1):
                k = jnp.where(quarter == v, row_of(coefs[v], j, SUBS), k)
            w = jnp.where(upper, row_of(weights[0], j, SUBS), row_of(weights[1], j, SUBS))
            both = row_of(own + other, nvar, SUBS)
            flux = k * (other - own) / (1.0 + k * both) * w
            main = flux.astype(BF16).astype(F32)
            terms.append(jnp.concatenate([main, flux - main], axis=0).astype(BF16))
            sources.append(
                jnp.concatenate([highs[j], highs[j]], axis=0).astype(F32).astype(BF16)
            )

        def add(group, carry):
            none = jnp.zeros((16, LANES), BF16)
            columns = []
            for j in range(SUBS):
                columns.append(
                    jnp.concatenate(
                        [
                            jnp.where(
                                sources[j]
                                == jnp.full((16, LANES), group * SUBS + k, jnp.int32)
                                .astype(F32)
                                .astype(BF16),
                                terms[j],
                                none,
                            )
                            for k in range(SUBS)
                        ],
                        axis=0,
                    )
                )
            a = jnp.concatenate(columns, axis=1)
            for c in range(2):
                acc[c, group] += contract_lanes(a, hots[c, step])
            return carry

        loop(groups, add, 0)
        return carry

    lax.fori_loop(0, half // SUBS, rows_step, 0, unroll=8)

    def give_back(group, carry):
        for c in range(2):
            for k in range(SUBS):
                base = 16 * k + 4 * c
                total = acc[c, group, base : base + 4, :] + acc[c, group, base + 8 : base + 12, :]
                ret_out[c * owners + group * SUBS + k] = total
        return carry

    loop(groups, give_back, 0)
    ret_in[me] = ret_out[me]
    spread_lists(ret_out, ret_in, 2, 3, False)

    wait_halos(1)
    smooth(1, once, dif, tr)

    slope = surface[nvar]
    gain[nlev - 1] = slope
    for level in range(nlev - 2, -1, -1):
        slope = fac[level] * slope
        gain[level] = slope
    for var in range(nvar):
        last = var * nlev + nlev - 1
        column = surface[var]
        off[last] = column + dif[last]
        for level in range(nlev - 2, -1, -1):
            n = var * nlev + level
            column = off[n] + fac[level] * column
            off[n] = column + dif[n]

    cells[...] = jnp.zeros_like(cells)
    wait_lists(ret_in, 3)

    def cells_step(group, carry):
        start = pl.multiple_of(group * SUBS, SUBS)
        cell = send_cell[pl.ds(start, SUBS), :]
        high = cell >> 7
        columns = []
        for j in range(SUBS):
            value = ret_in[start + j] + ret_in[owners + start + j]
            mask = row_of(high, j, SUBS) == sub8
            parts = []
            for _ in range(3):
                part = value.astype(BF16).astype(F32)
                value = value - part
                for v in range(4):
                    parts.append(jnp.where(mask, row_of(part, v, SUBS), 0.0))
            columns.append(jnp.concatenate(parts, axis=0).astype(BF16))
        cells[...] += contract_lanes(
            jnp.concatenate(columns, axis=1), cell_hots[group]
        )
        return carry

    loop(groups, cells_step, 0)
    for var in range(nvar):
        parts = [cells[32 * k + 8 * var : 32 * k + 8 * var + 8, :] for k in range(3)]
        flux = parts[0] + (parts[1] + parts[2])
        for level in range(nlev):
            n = var * nlev + level
            out[n] = off[n] + gain[level] * flux

    for copy in part_copies:
        copy.wait_send()
    finish_halos(0)
    finish_halos(1)
    wait_lists(tab_in, 0)
    wait_lists(ret_in, 2)


def per_device(
    n_tile, n_sub, tracers, couple, send_cell, recv_pos, row_count, sea_mask, exch_coef, margin_area
):
    nvar, nlev = tracers.shape[1:3]
    tiles = nvar * nlev
    owners = n_tile * n_sub
    rows = recv_pos.shape[-1] // LANES
    slab = tiles // SUBS
    block = (SUBS, LANES)
    vmem = pl.BlockSpec(memory_space=pltpu.VMEM)
    hbm = pl.BlockSpec(memory_space=pltpu.HBM)
    scratch = [
        pltpu.VMEM((tiles,) + block, F32),
        pltpu.VMEM((nlev,) + block, F32),
        pltpu.VMEM((owners, LANES), jnp.int32),
        pltpu.VMEM((rows // 2, LANES), jnp.int32),
        pltpu.VMEM((nvar, rows // 2, LANES), F32),
        pltpu.SemaphoreType.DMA((7,)),
        pltpu.VMEM((tiles,) + block, F32),
        pltpu.VMEM((nlev,) + block, F32),
        pltpu.VMEM((tiles,) + block, F32),
        pltpu.VMEM((tiles,) + block, F32),
        pltpu.VMEM((nlev,) + block, F32),
        pltpu.VMEM((2, rows // 2 // SUBS, LANES, SUBS * LANES), BF16),
        pltpu.VMEM((owners // SUBS, LANES, SUBS * LANES), BF16),
        pltpu.VMEM((owners, 4, LANES), F32),
        pltpu.VMEM((2 * owners, 4, LANES), F32),
        pltpu.VMEM((owners,) + block, F32),
        pltpu.VMEM((2, rows // 2, LANES), jnp.int32),
        pltpu.VMEM((2, rows // 2, LANES), F32),
        pltpu.VMEM((2, rows // 2, LANES), F32),
        pltpu.VMEM((2, owners // SUBS, 16 * SUBS, LANES), F32),
        pltpu.VMEM((2 * owners, 4, LANES), F32),
        pltpu.VMEM((2 * owners, 4, LANES), F32),
        pltpu.VMEM((2, 2, slab) + block, F32),
        pltpu.VMEM((2, 2, slab) + block, F32),
        pltpu.VMEM((2, 2) + block, F32),
        pltpu.VMEM((2, 2) + block, F32),
        pltpu.VMEM((96, LANES), F32),
        pltpu.SemaphoreType.DMA((4,)),
        pltpu.SemaphoreType.DMA((2, 4)),
        pltpu.SemaphoreType.DMA((2, 4)),
        pltpu.SemaphoreType.DMA((4,)),
    ]
    updated = pl.pallas_call(
        functools.partial(kernel, n_tile, n_sub, nvar, nlev),
        out_shape=jax.ShapeDtypeStruct((tiles,) + block, F32),
        in_specs=[hbm] * 4 + [pl.BlockSpec(memory_space=pltpu.SMEM)] + [hbm] * 3,
        out_specs=vmem,
        scratch_shapes=scratch,
        compiler_params=pltpu.CompilerParams(
            collective_id=0, has_side_effects=True, vmem_limit_bytes=40 * 1024 * 1024
        ),
        name="coupled_step",
    )(
        pltpu.with_memory_space_constraint(tracers.reshape((tiles,) + block), pltpu.HBM),
        pltpu.with_memory_space_constraint(couple.reshape((nlev,) + block), pltpu.HBM),
        pltpu.with_memory_space_constraint(send_cell.reshape(owners, LANES), pltpu.HBM),
        pltpu.with_memory_space_constraint(recv_pos.reshape(rows, LANES), pltpu.HBM),
        row_count,
        pltpu.with_memory_space_constraint(sea_mask.reshape(rows, LANES), pltpu.HBM),
        pltpu.with_memory_space_constraint(exch_coef.reshape(nvar, rows, LANES), pltpu.HBM),
        pltpu.with_memory_space_constraint(margin_area.reshape(rows, LANES), pltpu.HBM),
    )
    return updated.reshape(tracers.shape)


def solution(mesh):
    placed = (
        P("comp", "member", None, "tile", "sub"),
        P("comp", "member", "tile", "sub"),
        P("comp", ("tile", "sub"), None, None),
        P("comp", ("tile", "sub"), None),
        P(("tile", "sub")),
        P(("tile", "sub"), None),
        P("member", ("tile", "sub"), None),
        P("comp", ("tile", "sub"), None),
    )
    return jax.shard_map(
        functools.partial(per_device, mesh.shape["tile"], mesh.shape["sub"]),
        mesh=mesh,
        in_specs=placed,
        out_specs=P("comp", "member", None, "tile", "sub"),
        check_vma=False,
    )
```
